32 devices in a mesh: groups: 2 (over y), expert: 4 (over x, core), narrow: 4 (over z).
Axes of the slice: x: 2, y: 2, z: 4, core: 2. Of those that a mesh axis runs over, the one named last changes fastest.
Arguments:
- tokens: bfloat16 [512, 3584], P(('groups', 'expert', 'narrow')), parts along dimension 0, may hold values from -6 to 6
- expert_ids: int32 [512, 8], P(('groups', 'expert')), parts along dimension 0, may hold values from 0 to 15, all different within a row; in each aligned block of 64 rows (0 to 63, 64 to 127, ...) at most 48 rows name the same one
- route_weights: float32 [512, 8], P(('groups', 'expert')), parts along dimension 0, may hold values from 0.05 to 0.4
- pair_flags: int32 [256], P(('groups', 'expert', 'narrow')), parts along dimension 0, may hold values 0 or 1
- shared_gate_up: bfloat16 [3584, 2, 2048], P(None, None, 'narrow'), may hold values from -0.09375 to 0.09375
- shared_down: bfloat16 [2048, 3584], P('narrow'), may hold values from -0.125 to 0.125
- expert_gate_up: bfloat16 [16, 3584, 2, 2048], P('expert', None, None, 'narrow'), may hold values from -0.09375 to 0.09375
- expert_down: bfloat16 [16, 2048, 3584], P('expert', 'narrow'), may hold values from -0.125 to 0.125
- readout: float32 [3584], replicated, may hold values from -0.09375 to 0.09375
Outputs:
- mixed: bfloat16 [512, 3584], P(('groups', 'expert', 'narrow')), parts along dimension 0
- pmi_scores: float32 [256], P(('groups', 'expert', 'narrow')), parts along dimension 0
The draws below stay inside these ranges and needn't reach their ends.
There are 2 independent parts, one for each index of `groups`. The reference program is written for one: setup_inputs(seed, part) draws one part's arguments, and reference() takes and returns one part's arrays. A program takes and returns all parts, laid end to end along the dimension named above; an argument that names none is the same for every part. Nothing has to cross between parts.
Inputs may be any that keep to these rules, and one draw needn't show every extreme that they name: `expert_ids`: each row names 8 different experts. In each aligned block of 64 rows no expert is named by more than 48 rows, a bound that some block reaches.
All inputs are finite; a program needn't handle non-finite values. Where the reference program divides by a largest or mean magnitude, that divisor is 1e-20 or more. No bound on the sum of `pair_flags` on one device may be relied on, other than what follows from the above.
Results may differ from the reference program's by a relative error of at most 0.012.
Values may be sent and summed in bfloat16 or wider, within the bound.
No kernel may reach another device: no remote copies, remote signals or barrier semaphores. Data moves between devices by JAX's collectives and lax.ppermute only.
A program may use at most 192 MiB of HBM per device.

```python
import math
import jax
import jax.numpy as jnp
import numpy as np
from jax import lax

D = 3584
FF = 2048
FF_SH = 2048
TOPK = 8
ROT = 128
ROWS_E = 64
EXPERTS = 16
TOKENS = 256
CAP = 48
N_EXPERT = 4
N_NARROW = 4


def plant(values, stream_key, least, top_value):
    spot = [jax.random.randint(jax.random.fold_in(stream_key, axis), (), 0, length) for axis, length in enumerate(values.shape)]
    main_axis = values.shape.index(max(values.shape))
    neighbour = spot[:main_axis] + [(spot[main_axis] + 1) % values.shape[main_axis]] + spot[main_axis + 1:]
    return values.at[tuple(spot)].set(least).at[tuple(neighbour)].set(top_value)


def shard_levels(key, extent, split, least, largest):
    def one(axis_at, shards_of):
        draws = jax.random.uniform(jax.random.fold_in(jax.random.fold_in(key, 6), axis_at), (shards_of,), jnp.float32, least / len(split), largest / len(split))
        return jnp.repeat(jnp.exp(draws), extent[axis_at] // shards_of).reshape((-1,) + (1,) * (len(extent) - axis_at - 1))

    loudness = one(*split[0])
    for cut in split[1:]:
        loudness = loudness * one(*cut)
    return loudness


def deal_out(stream_key, own, number, rows, count, top, most, slope):
    sequence = jax.random.permutation(stream_key, count)
    packed, ordinary = shares(count, rows * top, most, slope, True), shares(count, rows * top, most, slope, False)
    places = jnp.arange(count)

    def named(tallies, rotation):
        used = int((tallies > 0).sum())
        fixed = max(1, used // 4)
        passed = fixed + (places - fixed + rotation * (used - fixed)) % max(1, count - fixed)
        return jnp.zeros((count,), jnp.int32).at[sequence[jnp.where(places < fixed, places, passed)]].set(jnp.asarray(tallies, jnp.int32))

    tallies = jnp.where(number % 4 == 0, named(packed, number // 4), named(ordinary, number - number // 4 - 1))
    mixed = jax.random.permutation(jax.random.fold_in(own, 3), count)
    donor, sink = mixed[0:count // 2 * 2:2], mixed[1:count // 2 * 2:2]
    slack = jnp.minimum(tallies[donor] - 1, most - tallies[sink]) // 2
    slack = jnp.where((donor == sequence[0]) | (sink == sequence[0]) | (tallies[sink] == 0), 0, jnp.maximum(slack, 0))
    passed = jax.random.randint(jax.random.fold_in(own, 4), (count // 2,), 0, 1 << 20) % (slack + 1)
    tallies = tallies.at[donor].add(-passed).at[sink].add(passed)
    labels = jnp.searchsorted(jnp.cumsum(tallies), jnp.arange(rows * top), side="right").astype(jnp.int32)
    grid = labels.reshape(top, rows).T
    grid = grid[jax.random.permutation(jax.random.fold_in(own, 1), rows)]
    rotation = jax.random.randint(jax.random.fold_in(own, 2), (rows, 1), 0, top)
    return jnp.take_along_axis(grid, (jnp.arange(top)[None, :] + rotation) % top, axis=1)


def shares(count, total, bound, skew, full):
    loads = [(1 << 20) // math.isqrt(grade ** skew) + 1 for grade in range(1, count + 1)]
    largest = bound if full else min(bound, max(-(-total // count), total * loads[0] // sum(loads)))
    least = 1 if total - largest >= count - 1 else 0
    counts, rest = [largest] + [least] * (count - 1), total - largest - least * (count - 1)
    while rest > 0:
        free = [i for i in range(1, count) if counts[i] < largest] or [i for i in range(1, count) if counts[i] < bound]
        whole, budget = sum([loads[i] for i in free]), rest
        for i in free:
            addition = min(bound - counts[i], max(1, budget * loads[i] // whole), rest)
            counts[i] = counts[i] + addition
            rest = rest - addition
    return np.array(counts)


def noise(stream_key, dims, spread, reach, cuts=(), held_as=jnp.bfloat16):
    values = spread * jax.random.normal(stream_key, dims, jnp.float32)
    if cuts:
        values = values * shard_levels(stream_key, dims, cuts, -0.22, 0.18)
    return jnp.clip(values, -reach, reach).astype(held_as)


def setup_inputs(seed: int = 0, part: int = 0) -> dict:
    streams_of = jax.random.split(jax.random.key(seed), 10)
    part_keys = jax.random.split(jax.random.fold_in(streams_of[9], part), 10)
    tokens = noise(part_keys[0], (TOKENS, D), 1.0, 6.0, ((0, 16),))
    expert_ids_keys = jax.random.split(jax.random.fold_in(part_keys[1], 1), TOKENS // ROWS_E)
    expert_ids_turns = jax.random.permutation(jax.random.fold_in(part_keys[1], 3), TOKENS // ROWS_E)
    expert_ids = jax.vmap(lambda own, number: deal_out(jax.random.fold_in(part_keys[1], 2), own, number, ROWS_E, EXPERTS, TOPK, CAP, 2))(expert_ids_keys, expert_ids_turns).reshape((TOKENS, TOPK))
    route_weights = jnp.clip(0.05 + 0.35 * jax.random.uniform(part_keys[2], (TOKENS, TOPK), jnp.float32) ** shard_levels(part_keys[2], (TOKENS, TOPK), ((0, 4),), -0.2, 0.2), 0.05, 0.4)
    pair_flags = plant((jax.random.randint(part_keys[3], (TOKENS // 2,), 0, 2) < 1).astype(jnp.int32), jax.random.fold_in(part_keys[3], 1), 0, 1)
    shared_gate_up = noise(streams_of[4], (D, 2, FF_SH), D ** -0.5, 0.09375, ((2, 4),))
    shared_down = noise(streams_of[5], (FF_SH, D), FF_SH ** -0.5, 0.125, ((0, 4),))
    expert_gate_up = noise(streams_of[6], (EXPERTS, D, 2, FF), D ** -0.5, 0.09375, ((0, 4), (3, 4)))
    expert_down = noise(streams_of[7], (EXPERTS, FF, D), FF ** -0.5, 0.125, ((0, 4), (1, 4)))
    readout = noise(streams_of[8], (D,), D ** -0.5, 0.09375, (), jnp.float32)
    return {"tokens": tokens, "expert_ids": expert_ids, "route_weights": route_weights, "pair_flags": pair_flags, "shared_gate_up": shared_gate_up, "shared_down": shared_down, "expert_gate_up": expert_gate_up, "expert_down": expert_down, "readout": readout}


def sign_matrix():
    row_index = lax.broadcasted_iota(jnp.int32, (ROT, ROT), 0)
    col_index = lax.broadcasted_iota(jnp.int32, (ROT, ROT), 1)
    common = jnp.bitwise_and(row_index, col_index)
    parity = jnp.zeros((ROT, ROT), jnp.int32)
    for shift_bits in range(ROT.bit_length() - 1):
        parity = parity + jnp.bitwise_and(jnp.right_shift(common, shift_bits), 1)
    return (1 - 2 * jnp.bitwise_and(parity, 1)).astype(jnp.bfloat16)

def quantize(member_rows):
    row_count = member_rows.shape[0]
    blocks = member_rows.reshape(row_count * (D // ROT), ROT)
    rotated = jnp.dot(blocks, sign_matrix(), preferred_element_type=jnp.float32) * (1.0 / math.sqrt(ROT))
    rotated = rotated.reshape(row_count, D // ROT, ROT)
    block_scale = (lax.optimization_barrier(jnp.max(jnp.abs(rotated), axis=2)) + 1e-06).astype(jnp.bfloat16)
    quantized = (rotated / block_scale.astype(jnp.float32)[:, :, None]).astype(jnp.bfloat16)
    return (quantized, block_scale)

def reference(tokens, expert_ids, route_weights, pair_flags, shared_gate_up, shared_down, expert_gate_up, expert_down, readout):
    quantized, block_scale = quantize(tokens)
    dequantized = (quantized.astype(jnp.float32) * block_scale.astype(jnp.float32)[:, :, None]).astype(jnp.bfloat16).reshape(TOKENS, D)
    capacity = N_EXPERT * CAP
    slice_len = FF // N_NARROW

    def one_expert(accumulated, inputs):
        gate_up, down, expert_index = inputs
        hit_mask = expert_ids == expert_index
        member = jnp.any(hit_mask, axis=1).astype(jnp.int32)
        members_first = jnp.argsort(1 - member, stable=True)[:capacity].astype(jnp.int32)
        member_rows = dequantized[members_first]
        gate_up_out = jnp.dot(member_rows, gate_up.reshape(D, 2 * FF), preferred_element_type=jnp.float32).reshape(capacity, 2, FF)
        hidden = (jax.nn.silu(gate_up_out[:, 0]) * gate_up_out[:, 1]).astype(jnp.bfloat16)
        result = jnp.zeros((capacity, D), jnp.float32)
        for slice_index in range(N_NARROW):
            lower = slice_index * slice_len
            part_out = jnp.dot(hidden[:, lower:lower + slice_len], down[lower:lower + slice_len], preferred_element_type=jnp.float32).astype(jnp.bfloat16)
            result = result + part_out.astype(jnp.float32)
        weight = lax.optimization_barrier(jnp.sum(jnp.where(hit_mask, route_weights, jnp.zeros_like(route_weights)), axis=1))[members_first]
        return (accumulated.at[members_first].add(weight[:, None] * result), None)
    routed, _ = lax.scan(one_expert, jnp.zeros((TOKENS, D), jnp.float32), (expert_gate_up, expert_down, jnp.arange(EXPERTS, dtype=jnp.int32)))
    shared_both = jnp.dot(tokens, shared_gate_up.reshape(D, 2 * FF_SH), preferred_element_type=jnp.float32).reshape(TOKENS, 2, FF_SH)
    shared_hidden = (jax.nn.silu(shared_both[:, 0]) * shared_both[:, 1]).astype(jnp.bfloat16)
    total_sum = jnp.dot(shared_hidden, shared_down, preferred_element_type=jnp.float32) + routed
    mixed = total_sum.astype(jnp.bfloat16)
    row_score = lax.optimization_barrier(jnp.sum(total_sum * readout[None, :], axis=1)) / jnp.sqrt(lax.optimization_barrier(jnp.mean(total_sum * total_sum, axis=1)) + 1e-06)
    paired = row_score.reshape(TOKENS // 2, 2)
    pmi_scores = (paired[:, 0] - paired[:, 1]) * (1 - 2 * pair_flags).astype(jnp.float32)
    return (mixed, pmi_scores)
```

```python
import functools
import math

import jax
import jax.numpy as jnp
from jax import lax
from jax.experimental import pallas as pl
from jax.experimental.pallas import tpu as pltpu
from jax.sharding import PartitionSpec as P

ROT = 128
CORES = 2
VMEM_BYTES = 30 * 1024 * 1024
SCATTER_CHUNKS = 2


def sign_matrix(copies):
    size = copies * ROT
    row_index = lax.broadcasted_iota(jnp.int32, (size, size), 0)
    col_index = lax.broadcasted_iota(jnp.int32, (size, size), 1)
    common = jnp.bitwise_and(row_index % ROT, col_index % ROT)
    parity = jnp.zeros((size, size), jnp.int32)
    for shift_bits in range(ROT.bit_length() - 1):
        parity = parity + jnp.bitwise_and(jnp.right_shift(common, shift_bits), 1)
    signs = 1 - 2 * jnp.bitwise_and(parity, 1)
    return jnp.where(row_index // ROT == col_index // ROT, signs, 0).astype(jnp.bfloat16)


def hidden_kernel(n_pieces, n_tiles, n_local, *refs):
    pieces = refs[:n_pieces]
    select, signs, gate_up, shared, hidden, shared_hidden, rows_s, deq_s, combine_s = refs[n_pieces:]
    step = pl.program_id(0)
    feature_len = deq_s.shape[1]
    width = signs.shape[0]

    @pl.when(step == 0)
    def _():
        base = 0
        for piece in pieces:
            count = piece.shape[0]
            rows_s[base : base + count, :] = piece[:, :feature_len]
            combine_s[base : base + count, :] = piece[:, feature_len:].astype(jnp.float32)
            base += count

        def block(index, carry):
            at = pl.ds(pl.multiple_of(index * width, width), width)
            rotated = jnp.dot(
                rows_s[:, at], signs[...], preferred_element_type=jnp.float32
            ) * (1.0 / math.sqrt(ROT))
            parts = []
            for piece_at in range(0, width, ROT):
                part = rotated[:, piece_at : piece_at + ROT]
                scale = (jnp.max(jnp.abs(part), axis=1, keepdims=True) + 1e-06).astype(jnp.bfloat16)
                scale = scale.astype(jnp.float32)
                quantized = (part / scale).astype(jnp.bfloat16)
                parts.append((quantized.astype(jnp.float32) * scale).astype(jnp.bfloat16))
            deq_s[:, at] = jnp.concatenate(parts, axis=1)
            return carry

        lax.fori_loop(0, feature_len // width, block, 0)
        gate = jnp.dot(rows_s[...], shared[0], preferred_element_type=jnp.float32)
        up = jnp.dot(rows_s[...], shared[1], preferred_element_type=jnp.float32)
        shared_hidden[...] = (gate / (1.0 + jnp.exp(-gate)) * up).astype(jnp.bfloat16)

    gate = jnp.dot(deq_s[...], gate_up[0, 0], preferred_element_type=jnp.float32)
    up = jnp.dot(deq_s[...], gate_up[0, 1], preferred_element_type=jnp.float32)
    local = step // (n_tiles // n_local)
    weight = jnp.sum(combine_s[...] * select[pl.ds(local, 1), :], axis=1, keepdims=True)
    hidden[...] = (gate / (1.0 + jnp.exp(-gate)) * up * weight).astype(jnp.bfloat16)


def hidden_rows(pieces, select, gate_up, shared):
    n_local, _, feature_len, inner = gate_up.shape
    rows = sum(piece.shape[0] for piece in pieces)
    signs = sign_matrix(2 if feature_len % (2 * ROT) == 0 else 1)
    tile = min(inner, 256)
    per = inner // tile
    whole = pl.BlockSpec(memory_space=pltpu.VMEM)
    return pl.pallas_call(
        functools.partial(hidden_kernel, len(pieces), n_local * per, n_local),
        grid=(n_local * per,),
        in_specs=[whole] * (len(pieces) + 2)
        + [pl.BlockSpec((1, 2, feature_len, tile), lambda s: (s // per, 0, 0, s % per)), whole],
        out_specs=[pl.BlockSpec((rows, tile), lambda s: (0, s)), whole],
        out_shape=[
            jax.ShapeDtypeStruct((rows, n_local * inner), jnp.bfloat16),
            jax.ShapeDtypeStruct((rows, shared.shape[2]), jnp.bfloat16),
        ],
        scratch_shapes=[
            pltpu.VMEM((rows, feature_len), jnp.bfloat16),
            pltpu.VMEM((rows, feature_len), jnp.bfloat16),
            pltpu.VMEM((rows, select.shape[1]), jnp.float32),
        ],
        compiler_params=pltpu.CompilerParams(vmem_limit_bytes=VMEM_BYTES),
        name="hidden_rows",
    )(*pieces, select, signs, gate_up, shared)


def down_kernel(hidden, shared_hidden, down, shared_down, out):
    out[...] = (
        jnp.dot(hidden[...], down[...], preferred_element_type=jnp.float32)
        + jnp.dot(shared_hidden[...], shared_down[...], preferred_element_type=jnp.float32)
    ).astype(out.dtype)


def down_rows(hidden, shared_hidden, down, shared_down, start, stop):
    rows = hidden.shape[0]
    inner = down.shape[0]
    tile = math.gcd(512, math.gcd(start, stop - start))
    first = start // tile
    whole = pl.BlockSpec(memory_space=pltpu.VMEM)
    return pl.pallas_call(
        down_kernel,
        grid=((stop - start) // tile,),
        in_specs=[
            whole,
            whole,
            pl.BlockSpec((inner, tile), lambda s: (0, first + s)),
            pl.BlockSpec((shared_down.shape[0], tile), lambda s: (0, first + s)),
        ],
        out_specs=pl.BlockSpec((rows, tile), lambda s: (0, s)),
        out_shape=jax.ShapeDtypeStruct((rows, stop - start), jnp.bfloat16),
        compiler_params=pltpu.CompilerParams(vmem_limit_bytes=VMEM_BYTES),
        name="down_rows",
    )(hidden, shared_hidden, down, shared_down)


def exchange(value, axis, flip):
    return lax.ppermute(value, axis, [(i, i ^ flip) for i in range(lax.axis_size(axis))])


def per_device(
    tokens,
    expert_ids,
    route_weights,
    pair_flags,
    shared_gate_up,
    shared_down,
    expert_gate_up,
    expert_down,
    readout,
):
    own_rows, feature_len = tokens.shape
    n_local, _, _, inner = expert_gate_up.shape
    expert_count = lax.axis_size("expert")
    narrow_count = lax.axis_size("narrow")
    chips = expert_count // CORES
    experts = n_local * expert_count
    expert_at = lax.axis_index("expert")
    narrow_at = lax.axis_index("narrow")

    ids = lax.dynamic_slice_in_dim(expert_ids, narrow_at * own_rows, own_rows, 0)
    chosen = lax.dynamic_slice_in_dim(route_weights, narrow_at * own_rows, own_rows, 0)
    named = lax.broadcasted_iota(jnp.int32, (1, 1, experts), 2)
    combine = jnp.sum(jnp.where(ids[:, :, None] == named, chosen[:, :, None], 0.0), axis=1)
    high = combine.astype(jnp.bfloat16)
    low = (combine - high.astype(jnp.float32)).astype(jnp.bfloat16)
    columns = -(-2 * experts // 128) * 128
    lanes = jnp.pad(jnp.concatenate([high, low], axis=1), ((0, 0), (0, columns - 2 * experts)))
    sent = jnp.concatenate([tokens, lanes], axis=1)
    local_ids = expert_at * n_local + lax.broadcasted_iota(jnp.int32, (n_local, columns), 0)
    column = lax.broadcasted_iota(jnp.int32, (n_local, columns), 1)
    select = ((column == local_ids) | (column == local_ids + experts)).astype(jnp.float32)

    along_z = jnp.concatenate(
        [sent] + [exchange(sent, "narrow", flip) for flip in range(1, narrow_count)], axis=0
    )
    chip_parts = [along_z] + [
        exchange(along_z, "expert", flip * CORES) for flip in range(1, chips)
    ]
    core_parts = [exchange(part, "expert", 1) for part in chip_parts]

    shared_len = shared_down.shape[0]
    part_len = shared_len // expert_count
    gate_up = jnp.transpose(expert_gate_up, (0, 2, 1, 3))
    if part_len % 128 == 0:
        shared_in = lax.dynamic_slice_in_dim(shared_gate_up, expert_at * part_len, part_len, 2)
        shared_out = lax.dynamic_slice_in_dim(shared_down, expert_at * part_len, part_len, 0)
    else:
        mine = lax.broadcasted_iota(jnp.int32, (shared_len, 1), 0) // part_len == expert_at
        shared_in = shared_gate_up
        shared_out = jnp.where(mine, shared_down, jnp.zeros_like(shared_down))
    shared_in = jnp.transpose(shared_in, (1, 0, 2))

    hidden, shared_hidden = hidden_rows(chip_parts + core_parts, select, gate_up, shared_in)
    down = expert_down.reshape(n_local * inner, feature_len)

    half = own_rows * narrow_count * chips
    totals = []
    width = feature_len // SCATTER_CHUNKS
    for chunk in range(SCATTER_CHUNKS):
        part = down_rows(
            hidden, shared_hidden, down, shared_out, chunk * width, (chunk + 1) * width
        )
        near = exchange(part[half:], "expert", 1)
        by_core = part[:half].astype(jnp.float32) + near.astype(jnp.float32)
        by_core = by_core.reshape(chips, narrow_count * own_rows, width)
        by_chip = by_core[0]
        for flip in range(1, chips):
            by_chip = by_chip + exchange(
                by_core[flip].astype(jnp.bfloat16), "expert", flip * CORES
            ).astype(jnp.float32)
        by_chip = by_chip.reshape(narrow_count, own_rows, width)
        total = by_chip[0]
        for flip in range(1, narrow_count):
            total = total + exchange(
                by_chip[flip].astype(jnp.bfloat16), "narrow", flip
            ).astype(jnp.float32)
        totals.append(total)
    total_sum = jnp.concatenate(totals, axis=1)
    mixed = total_sum.astype(jnp.bfloat16)
    row_score = jnp.sum(total_sum * readout[None, :], axis=1) / jnp.sqrt(
        jnp.mean(total_sum * total_sum, axis=1) + 1e-06
    )
    paired = row_score.reshape(-1, 2)
    pmi_scores = (paired[:, 0] - paired[:, 1]) * (1 - 2 * pair_flags).astype(jnp.float32)
    return (mixed, pmi_scores)


def solution(mesh):
    in_specs = (
        P(("groups", "expert", "narrow"), None),
        P(("groups", "expert"), None),
        P(("groups", "expert"), None),
        P(("groups", "expert", "narrow")),
        P(None, None, "narrow"),
        P("narrow", None),
        P("expert", None, None, "narrow"),
        P("expert", "narrow", None),
        P(),
    )
    out_specs = (P(("groups", "expert", "narrow"), None), P(("groups", "expert", "narrow")))
    return jax.shard_map(
        per_device, mesh=mesh, in_specs=in_specs, out_specs=out_specs, check_vma=False
    )
```

```python
import functools
import math

import jax
import jax.numpy as jnp
from jax import lax
from jax.experimental import pallas as pl
from jax.experimental.pallas import tpu as pltpu
from jax.sharding import PartitionSpec as P

ROT = 128
CORES = 2
SMALL_VMEM = 12 * 1024 * 1024
VMEM_BYTES = 16 * 1024 * 1024
SCATTER_CHUNKS = 2


def sign_matrix(copies):
    size = copies * ROT
    row_index = lax.broadcasted_iota(jnp.int32, (size, size), 0)
    col_index = lax.broadcasted_iota(jnp.int32, (size, size), 1)
    common = jnp.bitwise_and(row_index % ROT, col_index % ROT)
    parity = jnp.zeros((size, size), jnp.int32)
    for shift_bits in range(ROT.bit_length() - 1):
        parity = parity + jnp.bitwise_and(jnp.right_shift(common, shift_bits), 1)
    signs = 1 - 2 * jnp.bitwise_and(parity, 1)
    return jnp.where(row_index // ROT == col_index // ROT, signs, 0).astype(jnp.bfloat16)


def in_vmem(value):
    return pltpu.with_memory_space_constraint(value, pltpu.VMEM)


def vmem(shape, dtype):
    return pltpu.VMEM(shape, dtype)


def apart_kernel(rows, chunk, *refs):
    source, out = refs[0], refs[-1]
    step = pl.program_id(0)
    count = 2 * out.shape[2] // 128
    for at in range(0, rows, chunk):
        pairs = source[0, at * count : (at + chunk) * count, :].reshape(chunk, count, 128)
        pairs = jnp.swapaxes(pairs, 0, 1)
        here = pl.ds(pl.multiple_of(step * rows + at, chunk), chunk)
        for q in range(count):
            out[q % 2, here, (q // 2) * 128 : (q // 2 + 1) * 128] = pairs[q]


def apart(packed, expert, feature_len, inner, after):
    count = 2 * inner // 128
    rows = feature_len // 4 if feature_len % 256 == 0 else feature_len
    chunk = 64 if rows % 64 == 0 else rows
    return pl.pallas_call(
        functools.partial(apart_kernel, rows, chunk),
        grid=(feature_len // rows,),
        in_specs=[pl.BlockSpec((1, rows * count, 128), lambda s: (expert, s, 0))]
        + [pl.BlockSpec(memory_space=pl.ANY)] * len(after),
        out_specs=pl.BlockSpec(memory_space=pltpu.VMEM),
        out_shape=vmem((2, feature_len, inner), packed.dtype),
        compiler_params=pltpu.CompilerParams(vmem_limit_bytes=SMALL_VMEM),
        cost_estimate=pl.CostEstimate(flops=0, bytes_accessed=1024, transcendentals=0),
        name="apart",
    )(packed, *after)


def join_kernel(n_pieces, *refs):
    lanes, out = refs[n_pieces], refs[-1]
    feature_len = refs[0].shape[1]
    base = 0
    for piece in refs[:n_pieces]:
        out[base : base + piece.shape[0], :feature_len] = piece[...]
        base += piece.shape[0]
    out[:, feature_len:] = lanes[...]


def join(pieces, lanes, after):
    whole = pl.BlockSpec(memory_space=pltpu.VMEM)
    return pl.pallas_call(
        functools.partial(join_kernel, len(pieces)),
        in_specs=[whole] * (len(pieces) + 1) + [pl.BlockSpec(memory_space=pl.ANY)] * len(after),
        out_specs=whole,
        out_shape=vmem((lanes.shape[0], pieces[0].shape[1] + lanes.shape[1]), lanes.dtype),
        compiler_params=pltpu.CompilerParams(vmem_limit_bytes=SMALL_VMEM),
        cost_estimate=pl.CostEstimate(flops=0, bytes_accessed=1024, transcendentals=0),
        name="join",
    )(*pieces, lanes, *after)


def rotate(source, signs, target, base):
    rows = source.shape[0]
    feature_len = target.shape[1]
    width = signs.shape[0]

    def block(index, carry):
        at = pl.ds(pl.multiple_of(index * width, width), width)
        rotated = jnp.dot(source[:, at], signs[...], preferred_element_type=jnp.float32) * (
            1.0 / math.sqrt(ROT)
        )
        parts = []
        for piece_at in range(0, width, ROT):
            part = rotated[:, piece_at : piece_at + ROT]
            scale = (jnp.max(jnp.abs(part), axis=1, keepdims=True) + 1e-06).astype(jnp.bfloat16)
            scale = scale.astype(jnp.float32)
            quantized = (part / scale).astype(jnp.bfloat16)
            parts.append((quantized.astype(jnp.float32) * scale).astype(jnp.bfloat16))
        target[base : base + rows, at] = jnp.concatenate(parts, axis=1)
        return carry

    lax.fori_loop(0, feature_len // width, block, 0)


def first_kernel(n_pieces, *refs):
    signs, out = refs[n_pieces:]
    base = 0
    for piece in refs[:n_pieces]:
        rotate(piece, signs, out, base)
        base += piece.shape[0]


def first_rows(pieces, signs, feature_len):
    whole = pl.BlockSpec(memory_space=pltpu.VMEM)
    rows = sum(piece.shape[0] for piece in pieces)
    return pl.pallas_call(
        functools.partial(first_kernel, len(pieces)),
        in_specs=[whole] * (len(pieces) + 1),
        out_specs=whole,
        out_shape=vmem((rows, feature_len), jnp.bfloat16),
        compiler_params=pltpu.CompilerParams(vmem_limit_bytes=SMALL_VMEM),
        cost_estimate=pl.CostEstimate(flops=0, bytes_accessed=1024, transcendentals=0),
        name="first_rows",
    )(*pieces, signs)


def rest_kernel(n_first, n_chips, *refs):
    n_pieces = CORES * n_chips
    pieces = refs[:n_pieces]
    signs, first, shared, deq, shared_hidden, combine, rows_s = refs[n_pieces:]
    count = pieces[0].shape[0]
    feature_len = deq.shape[1]
    for core in range(CORES):
        for chip in range(n_chips):
            base = (core * n_chips + chip) * count
            if chip == 0:
                piece = pieces[core]
                deq[base : base + count, :] = first[core * count : (core + 1) * count, :]
            else:
                piece = pieces[CORES + core * (n_chips - 1) + chip - 1]
                rotate(piece, signs, deq, base)
            rows_s[base : base + count, :] = piece[:, :feature_len]
            combine[base : base + count, :] = piece[:, feature_len:].astype(jnp.float32)
    part = shared.shape[1] // 2
    both = jnp.dot(rows_s[...], shared[...], preferred_element_type=jnp.float32)
    gate, up = both[:, :part], both[:, part:]
    shared_hidden[...] = (gate / (1.0 + jnp.exp(-gate)) * up).astype(jnp.bfloat16)


def rest_rows(pieces, signs, first, shared, n_chips):
    whole = pl.BlockSpec(memory_space=pltpu.VMEM)
    rows = sum(piece.shape[0] for piece in pieces)
    feature_len = first.shape[1]
    return pl.pallas_call(
        functools.partial(rest_kernel, len(pieces), n_chips),
        in_specs=[whole] * (len(pieces) + 3),
        out_specs=[whole] * 3,
        out_shape=[
            vmem((rows, feature_len), jnp.bfloat16),
            vmem((rows, shared.shape[1] // 2), jnp.bfloat16),
            vmem((rows, pieces[0].shape[1] - feature_len), jnp.float32),
        ],
        scratch_shapes=[pltpu.VMEM((rows, feature_len), jnp.bfloat16)],
        compiler_params=pltpu.CompilerParams(vmem_limit_bytes=SMALL_VMEM),
        name="rest_rows",
    )(*pieces, signs, first, shared)


def hidden_kernel(n_local, *refs):
    deq, combine, select = refs[:3]
    weights, out = refs[3 : 3 + n_local], refs[3 + n_local]
    inner = out.shape[1] // n_local
    for local in range(n_local):
        gate = jnp.dot(deq[...], weights[local][0], preferred_element_type=jnp.float32)
        up = jnp.dot(deq[...], weights[local][1], preferred_element_type=jnp.float32)
        weight = jnp.sum(combine[...] * select[local : local + 1, :], axis=1, keepdims=True)
        out[:, local * inner : (local + 1) * inner] = (
            gate / (1.0 + jnp.exp(-gate)) * up * weight
        ).astype(jnp.bfloat16)


def hidden_rows(deq, combine, select, weights):
    whole = pl.BlockSpec(memory_space=pltpu.VMEM)
    rows = deq.shape[0]
    return pl.pallas_call(
        functools.partial(hidden_kernel, len(weights)),
        in_specs=[whole] * (3 + len(weights)),
        out_specs=whole,
        out_shape=vmem((rows, len(weights) * weights[0].shape[2]), jnp.bfloat16),
        compiler_params=pltpu.CompilerParams(vmem_limit_bytes=SMALL_VMEM),
        name="hidden_rows",
    )(deq, combine, select, *weights)


def down_kernel(hidden, shared_hidden, down, shared_down, out):
    out[...] = (
        jnp.dot(hidden[...], down[...], preferred_element_type=jnp.float32)
        + jnp.dot(shared_hidden[...], shared_down[...], preferred_element_type=jnp.float32)
    ).astype(out.dtype)


def down_rows(hidden, shared_hidden, down, shared_down, start, stop):
    rows = hidden.shape[0]
    inner = down.shape[0]
    tile = math.gcd(512, math.gcd(start, stop - start))
    first = start // tile
    whole = pl.BlockSpec(memory_space=pltpu.VMEM)
    return pl.pallas_call(
        down_kernel,
        grid=((stop - start) // tile,),
        in_specs=[
            whole,
            whole,
            pl.BlockSpec((inner, tile), lambda s: (0, first + s)),
            pl.BlockSpec((shared_down.shape[0], tile), lambda s: (0, first + s)),
        ],
        out_specs=pl.BlockSpec((rows, tile), lambda s: (0, s)),
        out_shape=jax.ShapeDtypeStruct((rows, stop - start), jnp.bfloat16),
        compiler_params=pltpu.CompilerParams(vmem_limit_bytes=VMEM_BYTES),
        name="down_rows",
    )(hidden, shared_hidden, down, shared_down)


def exchange(value, axis, flip):
    return lax.ppermute(value, axis, [(i, i ^ flip) for i in range(lax.axis_size(axis))])


def per_device(
    tokens,
    expert_ids,
    route_weights,
    pair_flags,
    shared_gate_up,
    shared_down,
    expert_gate_up,
    expert_down,
    readout,
):
    own_rows, feature_len = tokens.shape
    n_local, _, _, inner = expert_gate_up.shape
    expert_count = lax.axis_size("expert")
    narrow_count = lax.axis_size("narrow")
    chips = expert_count // CORES
    experts = n_local * expert_count
    expert_at = lax.axis_index("expert")
    narrow_at = lax.axis_index("narrow")

    named = lax.broadcasted_iota(jnp.int32, (1, 1, experts), 2)
    combine = jnp.sum(
        jnp.where(expert_ids[:, :, None] == named, route_weights[:, :, None], 0.0), axis=1
    )
    high = combine.astype(jnp.bfloat16)
    low = (combine - high.astype(jnp.float32)).astype(jnp.bfloat16)
    columns = -(-2 * experts // 128) * 128
    lanes = jnp.pad(jnp.concatenate([high, low], axis=1), ((0, 0), (0, columns - 2 * experts)))
    lanes = lanes.reshape(narrow_count, own_rows, columns)
    order = narrow_at ^ jnp.arange(narrow_count)
    lanes = lanes[order].reshape(narrow_count * own_rows, columns)
    local_ids = expert_at * n_local + lax.broadcasted_iota(jnp.int32, (n_local, columns), 0)
    column = lax.broadcasted_iota(jnp.int32, (n_local, columns), 1)
    select = ((column == local_ids) | (column == local_ids + experts)).astype(jnp.float32)

    shared_len = shared_down.shape[0]
    part_len = shared_len // expert_count
    if part_len % 128 == 0:
        shared_in = lax.dynamic_slice_in_dim(shared_gate_up, expert_at * part_len, part_len, 2)
        shared_out = lax.dynamic_slice_in_dim(shared_down, expert_at * part_len, part_len, 0)
    else:
        mine = lax.broadcasted_iota(jnp.int32, (shared_len, 1), 0) // part_len == expert_at
        shared_in = shared_gate_up
        shared_out = jnp.where(mine, shared_down, jnp.zeros_like(shared_down))
    shared_in = shared_in.reshape(feature_len, -1)
    signs = sign_matrix(2 if feature_len % (2 * ROT) == 0 else 1)

    packed = expert_gate_up.reshape(n_local, feature_len, 2, inner // 128, 128)
    packed = packed.transpose(0, 1, 3, 2, 4).reshape(n_local, -1, 128)
    packed = pltpu.with_memory_space_constraint(packed, pltpu.HBM)

    def prepared(expert, after):
        return apart(packed, expert, feature_len, inner, after)

    early = (n_local + 1) // 2
    from_z = [exchange(tokens, "narrow", flip) for flip in range(1, narrow_count)]
    weights = []
    for expert in range(early):
        weights.append(prepared(expert, weights[-1:]))
    along_z = join([tokens] + from_z, lanes, weights[-1:])
    from_x = [exchange(along_z, "expert", flip * CORES) for flip in range(1, chips)]
    near = exchange(along_z, "expert", 1)
    first = first_rows([along_z, near], signs, feature_len)
    after = [along_z]
    for expert in range(early, n_local):
        weights.append(prepared(expert, after))
        after = weights[-1:]
    from_both = [exchange(part, "expert", 1) for part in from_x]

    deq, shared_hidden, combine = rest_rows(
        [along_z, near] + from_x + from_both, signs, first, shared_in, chips
    )
    hidden = hidden_rows(deq, combine, select, weights)
    down = expert_down.reshape(n_local * inner, feature_len)

    half = own_rows * narrow_count * chips
    totals = []
    width = feature_len // SCATTER_CHUNKS
    for chunk in range(SCATTER_CHUNKS):
        part = down_rows(
            hidden, shared_hidden, down, shared_out, chunk * width, (chunk + 1) * width
        )
        near = exchange(part[half:], "expert", 1)
        by_core = part[:half].astype(jnp.float32) + near.astype(jnp.float32)
        by_core = by_core.reshape(chips, narrow_count * own_rows, width)
        by_chip = by_core[0]
        for flip in range(1, chips):
            by_chip = by_chip + exchange(
                by_core[flip].astype(jnp.bfloat16), "expert", flip * CORES
            ).astype(jnp.float32)
        by_chip = by_chip.reshape(narrow_count, own_rows, width)
        total = by_chip[0]
        for flip in range(1, narrow_count):
            total = total + exchange(
                by_chip[flip].astype(jnp.bfloat16), "narrow", flip
            ).astype(jnp.float32)
        totals.append(total)
    total_sum = jnp.concatenate(totals, axis=1)
    mixed = total_sum.astype(jnp.bfloat16)
    row_score = jnp.sum(total_sum * readout[None, :], axis=1) / jnp.sqrt(
        jnp.mean(total_sum * total_sum, axis=1) + 1e-06
    )
    paired = row_score.reshape(-1, 2)
    pmi_scores = (paired[:, 0] - paired[:, 1]) * (1 - 2 * pair_flags).astype(jnp.float32)
    return (mixed, pmi_scores)


def solution(mesh):
    in_specs = (
        P(("groups", "expert", "narrow"), None),
        P(("groups", "expert"), None),
        P(("groups", "expert"), None),
        P(("groups", "expert", "narrow")),
        P(None, None, "narrow"),
        P("narrow", None),
        P("expert", None, None, "narrow"),
        P("expert", "narrow", None),
        P(),
    )
    out_specs = (P(("groups", "expert", "narrow"), None), P(("groups", "expert", "narrow")))
    return jax.shard_map(
        per_device, mesh=mesh, in_specs=in_specs, out_specs=out_specs, check_vma=False
    )
```

```python
import functools
import math

import jax
import jax.numpy as jnp
from jax import lax
from jax.experimental import pallas as pl
from jax.experimental.pallas import tpu as pltpu
from jax.sharding import PartitionSpec as P

ROT = 128
CORES = 2
SMALL_VMEM = 10 * 1024 * 1024
HIDDEN_VMEM = 5 * 1024 * 1024
VMEM_BYTES = 16 * 1024 * 1024


def sign_matrix(copies):
    size = copies * ROT
    row_index = lax.broadcasted_iota(jnp.int32, (size, size), 0)
    col_index = lax.broadcasted_iota(jnp.int32, (size, size), 1)
    common = jnp.bitwise_and(row_index % ROT, col_index % ROT)
    parity = jnp.zeros((size, size), jnp.int32)
    for shift_bits in range(ROT.bit_length() - 1):
        parity = parity + jnp.bitwise_and(jnp.right_shift(common, shift_bits), 1)
    signs = 1 - 2 * jnp.bitwise_and(parity, 1)
    return jnp.where(row_index // ROT == col_index // ROT, signs, 0).astype(jnp.bfloat16)


def in_vmem(value):
    return pltpu.with_memory_space_constraint(value, pltpu.VMEM)


def vmem(shape, dtype):
    return pltpu.VMEM(shape, dtype)


def apart_kernel(experts, rows, chunk, n_after, *refs):
    source = refs[0]
    outs = refs[1 + n_after : 1 + n_after + len(experts)]
    done, held, sems = refs[1 + n_after + len(experts) :]
    slots = held.shape[0]
    count = 2 * outs[0].shape[2] // 128
    pieces = [(n, step) for n in range(len(experts)) for step in range(outs[0].shape[1] // rows)]

    def copy(at):
        n, step = pieces[at]
        return pltpu.make_async_copy(
            source.at[experts[n], pl.ds(step * rows * count, rows * count)],
            held.at[at % slots],
            sems.at[at % slots],
        )

    for at in range(min(slots, len(pieces))):
        copy(at).start()
    for at, (n, step) in enumerate(pieces):
        copy(at).wait()
        for row in range(0, rows, chunk):
            pairs = held[at % slots, row * count : (row + chunk) * count, :]
            pairs = jnp.swapaxes(pairs.reshape(chunk, count, 128), 0, 1)
            here = slice(step * rows + row, step * rows + row + chunk)
            for q in range(count):
                outs[n][q % 2, here, (q // 2) * 128 : (q // 2 + 1) * 128] = pairs[q]
        if at + slots < len(pieces):
            copy(at + slots).start()
    done[...] = jnp.zeros_like(done)


def apart(packed, experts, feature_len, inner, after):
    count = 2 * inner // 128
    rows = feature_len // 4 if feature_len % 256 == 0 else feature_len
    chunk = 64 if rows % 64 == 0 else rows
    whole = pl.BlockSpec(memory_space=pltpu.VMEM)
    out = pl.pallas_call(
        functools.partial(apart_kernel, experts, rows, chunk, len(after)),
        in_specs=[pl.BlockSpec(memory_space=pl.ANY)] * (1 + len(after)),
        out_specs=[whole] * (len(experts) + 1),
        out_shape=[vmem((2, feature_len, inner), packed.dtype)] * len(experts)
        + [jax.ShapeDtypeStruct((8, 128), jnp.float32)],
        scratch_shapes=[
            pltpu.VMEM((4, rows * count, 128), packed.dtype),
            pltpu.SemaphoreType.DMA((4,)),
        ],
        compiler_params=pltpu.CompilerParams(vmem_limit_bytes=SMALL_VMEM),
        cost_estimate=pl.CostEstimate(flops=0, bytes_accessed=1024, transcendentals=0),
        name="apart",
    )(packed, *after)
    return out[:-1], out[-1]


def pass_kernel(value, *refs):
    refs[-1][...] = value[...]


def pass_on(value, after):
    return pl.pallas_call(
        pass_kernel,
        in_specs=[pl.BlockSpec(memory_space=pltpu.VMEM)]
        + [pl.BlockSpec(memory_space=pl.ANY)] * len(after),
        out_specs=pl.BlockSpec(memory_space=pltpu.VMEM),
        out_shape=vmem(value.shape, value.dtype),
        compiler_params=pltpu.CompilerParams(vmem_limit_bytes=HIDDEN_VMEM),
        cost_estimate=pl.CostEstimate(flops=0, bytes_accessed=1024, transcendentals=0),
        name="pass_on",
    )(value, *after)


def join_kernel(n_pieces, *refs):
    lanes, out = refs[n_pieces], refs[-1]
    feature_len = refs[0].shape[1]
    base = 0
    for piece in refs[:n_pieces]:
        out[base : base + piece.shape[0], :feature_len] = piece[...]
        base += piece.shape[0]
    out[:, feature_len:] = lanes[...]


def join(pieces, lanes, after):
    whole = pl.BlockSpec(memory_space=pltpu.VMEM)
    return pl.pallas_call(
        functools.partial(join_kernel, len(pieces)),
        in_specs=[whole] * (len(pieces) + 1) + [pl.BlockSpec(memory_space=pl.ANY)] * len(after),
        out_specs=whole,
        out_shape=vmem((lanes.shape[0], pieces[0].shape[1] + lanes.shape[1]), lanes.dtype),
        compiler_params=pltpu.CompilerParams(vmem_limit_bytes=HIDDEN_VMEM),
        cost_estimate=pl.CostEstimate(flops=0, bytes_accessed=1024, transcendentals=0),
        name="join",
    )(*pieces, lanes, *after)


def rotate(sources, signs, target, bases):
    feature_len = target.shape[1]
    width = signs.shape[0]
    for at in range(0, feature_len, width):
        for source, base in zip(sources, bases):
            rotated = jnp.dot(
                source[:, at : at + width], signs[...], preferred_element_type=jnp.float32
            ) * (1.0 / math.sqrt(ROT))
            for piece_at in range(0, width, ROT):
                part = rotated[:, piece_at : piece_at + ROT]
                scale = jnp.max(jnp.abs(part), axis=1, keepdims=True) + 1e-06
                scale = scale.astype(jnp.bfloat16).astype(jnp.float32)
                quantized = (part * (1.0 / scale)).astype(jnp.bfloat16).astype(jnp.float32)
                target[
                    base : base + source.shape[0], at + piece_at : at + piece_at + ROT
                ] = (quantized * scale).astype(jnp.bfloat16)


def first_kernel(n_pieces, *refs):
    signs, out = refs[n_pieces:]
    pieces = refs[:n_pieces]
    rotate(pieces, signs, out, [n * pieces[0].shape[0] for n in range(n_pieces)])


def first_rows(pieces, signs, feature_len):
    whole = pl.BlockSpec(memory_space=pltpu.VMEM)
    rows = sum(piece.shape[0] for piece in pieces)
    return pl.pallas_call(
        functools.partial(first_kernel, len(pieces)),
        in_specs=[whole] * (len(pieces) + 1),
        out_specs=whole,
        out_shape=vmem((rows, feature_len), jnp.bfloat16),
        compiler_params=pltpu.CompilerParams(vmem_limit_bytes=HIDDEN_VMEM),
        cost_estimate=pl.CostEstimate(flops=0, bytes_accessed=1024, transcendentals=0),
        name="first_rows",
    )(*pieces, signs)


def rest_kernel(n_first, n_chips, *refs):
    n_pieces = CORES * n_chips
    pieces = refs[:n_pieces]
    signs, first, shared, deq, shared_hidden, combine, rows_s = refs[n_pieces:]
    count = pieces[0].shape[0]
    feature_len = deq.shape[1]
    sources, bases = [], []
    for core in range(CORES):
        for chip in range(n_chips):
            base = (core * n_chips + chip) * count
            if chip == 0:
                piece = pieces[core]
                deq[base : base + count, :] = first[core * count : (core + 1) * count, :]
            else:
                piece = pieces[CORES + core * (n_chips - 1) + chip - 1]
                sources.append(piece)
                bases.append(base)
            rows_s[base : base + count, :] = piece[:, :feature_len]
            combine[base : base + count, :] = piece[:, feature_len:].astype(jnp.float32)
    rotate(sources, signs, deq, bases)
    part = shared.shape[1] // 2
    both = jnp.dot(rows_s[...], shared[...], preferred_element_type=jnp.float32)
    gate, up = both[:, :part], both[:, part:]
    shared_hidden[...] = (gate / (1.0 + jnp.exp(-gate)) * up).astype(jnp.bfloat16)


def rest_rows(pieces, signs, first, shared, n_chips):
    whole = pl.BlockSpec(memory_space=pltpu.VMEM)
    rows = sum(piece.shape[0] for piece in pieces)
    feature_len = first.shape[1]
    return pl.pallas_call(
        functools.partial(rest_kernel, len(pieces), n_chips),
        in_specs=[whole] * (len(pieces) + 3),
        out_specs=[whole] * 3,
        out_shape=[
            vmem((rows, feature_len), jnp.bfloat16),
            vmem((rows, shared.shape[1] // 2), jnp.bfloat16),
            vmem((rows, pieces[0].shape[1] - feature_len), jnp.float32),
        ],
        scratch_shapes=[pltpu.VMEM((rows, feature_len), jnp.bfloat16)],
        compiler_params=pltpu.CompilerParams(vmem_limit_bytes=HIDDEN_VMEM + 2 * rows * feature_len),
        name="rest_rows",
    )(*pieces, signs, first, shared)


def hidden_kernel(n_local, *refs):
    deq, combine, select = refs[:3]
    weights, out = refs[3 : 3 + n_local], refs[3 + n_local]
    inner = out.shape[1] // n_local
    for local in range(n_local):
        gate = jnp.dot(deq[...], weights[local][0], preferred_element_type=jnp.float32)
        up = jnp.dot(deq[...], weights[local][1], preferred_element_type=jnp.float32)
        weight = jnp.sum(combine[...] * select[local : local + 1, :], axis=1, keepdims=True)
        out[:, local * inner : (local + 1) * inner] = (
            gate / (1.0 + jnp.exp(-gate)) * up * weight
        ).astype(jnp.bfloat16)


def hidden_rows(deq, combine, select, weights):
    whole = pl.BlockSpec(memory_space=pltpu.VMEM)
    rows = deq.shape[0]
    return pl.pallas_call(
        functools.partial(hidden_kernel, len(weights)),
        in_specs=[whole] * (3 + len(weights)),
        out_specs=whole,
        out_shape=vmem((rows, len(weights) * weights[0].shape[2]), jnp.bfloat16),
        compiler_params=pltpu.CompilerParams(vmem_limit_bytes=HIDDEN_VMEM),
        name="hidden_rows",
    )(deq, combine, select, *weights)


def down_kernel(index, hidden, shared_hidden, down, shared_down, out):
    out[...] = (
        jnp.dot(hidden[...], down[...], preferred_element_type=jnp.float32)
        + jnp.dot(shared_hidden[...], shared_down[...], preferred_element_type=jnp.float32)
    ).astype(out.dtype)


def down_rows(index, hidden, shared_hidden, down, shared_down, start, stop):
    rows = hidden.shape[0]
    inner = down.shape[0]
    tile = math.gcd(512, math.gcd(start, stop - start))
    first = start // tile
    whole = pl.BlockSpec(memory_space=pltpu.VMEM)
    return pl.pallas_call(
        down_kernel,
        grid_spec=pltpu.PrefetchScalarGridSpec(
            num_scalar_prefetch=1,
            grid=((stop - start) // tile,),
            in_specs=[
                whole,
                whole,
                pl.BlockSpec((inner, tile), lambda s, at: (0, first + s)),
                pl.BlockSpec((shared_hidden.shape[1], tile), lambda s, at: (at[0], first + s)),
            ],
            out_specs=pl.BlockSpec((rows, tile), lambda s, at: (0, s)),
        ),
        out_shape=jax.ShapeDtypeStruct((rows, stop - start), jnp.bfloat16),
        compiler_params=pltpu.CompilerParams(vmem_limit_bytes=VMEM_BYTES),
        name="down_rows",
    )(index, hidden, shared_hidden, down, shared_down)


def exchange(value, axis, flip):
    return lax.ppermute(value, axis, [(i, i ^ flip) for i in range(lax.axis_size(axis))])


def per_device(
    tokens,
    expert_ids,
    route_weights,
    pair_flags,
    shared_gate_up,
    shared_down,
    expert_gate_up,
    expert_down,
    readout,
):
    own_rows, feature_len = tokens.shape
    n_local, _, _, inner = expert_gate_up.shape
    expert_count = lax.axis_size("expert")
    narrow_count = lax.axis_size("narrow")
    chips = expert_count // CORES
    experts = n_local * expert_count
    expert_at = lax.axis_index("expert")
    narrow_at = lax.axis_index("narrow")

    named = lax.broadcasted_iota(jnp.int32, (1, 1, experts), 2)
    combine = jnp.sum(
        jnp.where(expert_ids[:, :, None] == named, route_weights[:, :, None], 0.0), axis=1
    )
    high = combine.astype(jnp.bfloat16)
    low = (combine - high.astype(jnp.float32)).astype(jnp.bfloat16)
    columns = -(-2 * experts // 128) * 128
    lanes = jnp.pad(jnp.concatenate([high, low], axis=1), ((0, 0), (0, columns - 2 * experts)))
    lanes = lanes.reshape(narrow_count, own_rows, columns)
    order = narrow_at ^ jnp.arange(narrow_count)
    lanes = lanes[order].reshape(narrow_count * own_rows, columns)
    local_ids = expert_at * n_local + lax.broadcasted_iota(jnp.int32, (n_local, columns), 0)
    column = lax.broadcasted_iota(jnp.int32, (n_local, columns), 1)
    select = ((column == local_ids) | (column == local_ids + experts)).astype(jnp.float32)

    shared_len = shared_down.shape[0]
    part_len = shared_len // expert_count
    if part_len % 128 == 0:
        shared_in = lax.dynamic_slice_in_dim(shared_gate_up, expert_at * part_len, part_len, 2)
        shared_out, index = shared_down, expert_at.reshape(1)
    else:
        mine = lax.broadcasted_iota(jnp.int32, (shared_len, 1), 0) // part_len == expert_at
        shared_in, index = shared_gate_up, jnp.zeros((1,), jnp.int32)
        shared_out = jnp.where(mine, shared_down, jnp.zeros_like(shared_down))
    shared_in = shared_in.reshape(feature_len, -1)
    signs = sign_matrix(2 if feature_len % (2 * ROT) == 0 else 1)

    packed = expert_gate_up.reshape(n_local, feature_len, 2, inner // 128, 128)
    packed = packed.transpose(0, 1, 3, 2, 4).reshape(n_local, -1, 128)
    packed = pltpu.with_memory_space_constraint(packed, pltpu.HBM)

    def prepared(experts, after):
        return apart(packed, experts, feature_len, inner, after)

    early = (n_local + 3) // 4
    from_z = [exchange(tokens, "narrow", flip) for flip in range(1, narrow_count)]
    weights, done = prepared(list(range(early)), [lanes, shared_in, select, signs, index])
    along_z = join([tokens] + from_z, lanes, [done])
    from_x = [exchange(along_z, "expert", flip * CORES) for flip in range(1, chips)]
    near = exchange(along_z, "expert", 1)
    after = [along_z]
    if n_local > early:
        late, done = prepared(list(range(early, n_local)), after)
        weights = weights + late
        after = [done]
    from_x = [pass_on(part, after) for part in from_x]
    from_both = [exchange(part, "expert", 1) for part in from_x]
    first = first_rows([along_z, near], signs, feature_len)

    deq, shared_hidden, combine = rest_rows(
        [along_z, near] + from_x + from_both, signs, first, shared_in, chips
    )
    down = pltpu.with_memory_space_constraint(
        expert_down.reshape(n_local * inner, feature_len), pltpu.HBM
    )
    hidden = hidden_rows(deq, combine, select, weights)

    half = own_rows * narrow_count * chips
    cut = feature_len * 5 // 14 // 256 * 256

    def by_core(start, stop):
        part = down_rows(index, hidden, shared_hidden, down, shared_out, start, stop)
        near = exchange(part[half:], "expert", 1)
        total = part[:half].astype(jnp.float32) + near.astype(jnp.float32)
        return total.reshape(chips, narrow_count, own_rows, stop - start)

    def add_up(parts, axis, step):
        total = parts[0]
        for flip in range(1, len(parts)):
            part = exchange(parts[flip].astype(jnp.bfloat16), axis, flip * step)
            total = total + part.astype(jnp.float32)
        return total

    totals = []
    if cut:
        parts = by_core(0, cut)
        parts = add_up(
            [parts[:, n].reshape(chips * own_rows, cut) for n in range(narrow_count)], "narrow", 1
        ).reshape(chips, own_rows, cut)
        totals.append(add_up([parts[c] for c in range(chips)], "expert", CORES))
    parts = by_core(cut, feature_len).reshape(chips, narrow_count * own_rows, feature_len - cut)
    parts = add_up([parts[c] for c in range(chips)], "expert", CORES)
    parts = parts.reshape(narrow_count, own_rows, feature_len - cut)
    totals.append(add_up([parts[n] for n in range(narrow_count)], "narrow", 1))
    total_sum = jnp.concatenate(totals, axis=1)
    mixed = total_sum.astype(jnp.bfloat16)
    row_score = jnp.sum(total_sum * readout[None, :], axis=1) / jnp.sqrt(
        jnp.mean(total_sum * total_sum, axis=1) + 1e-06
    )
    paired = row_score.reshape(-1, 2)
    pmi_scores = (paired[:, 0] - paired[:, 1]) * (1 - 2 * pair_flags).astype(jnp.float32)
    return (mixed, pmi_scores)


def solution(mesh):
    in_specs = (
        P(("groups", "expert", "narrow"), None),
        P(("groups", "expert"), None),
        P(("groups", "expert"), None),
        P(("groups", "expert", "narrow")),
        P(None, None, "narrow"),
        P("narrow", None),
        P("expert", None, None, "narrow"),
        P("expert", "narrow", None),
        P(),
    )
    out_specs = (P(("groups", "expert", "narrow"), None), P(("groups", "expert", "narrow")))
    return jax.shard_map(
        per_device, mesh=mesh, in_specs=in_specs, out_specs=out_specs, check_vma=False
    )
```

```python
import functools
import math

import jax
import jax.numpy as jnp
from jax import lax
from jax.experimental import pallas as pl
from jax.experimental.pallas import tpu as pltpu
from jax.sharding import PartitionSpec as P

ROT = 128
CORES = 2
SMALL_VMEM = 10 * 1024 * 1024
HIDDEN_VMEM = 5 * 1024 * 1024


def sign_matrix(copies):
    size = copies * ROT
    row_index = lax.broadcasted_iota(jnp.int32, (size, size), 0)
    col_index = lax.broadcasted_iota(jnp.int32, (size, size), 1)
    common = jnp.bitwise_and(row_index % ROT, col_index % ROT)
    parity = jnp.zeros((size, size), jnp.int32)
    for shift_bits in range(ROT.bit_length() - 1):
        parity = parity + jnp.bitwise_and(jnp.right_shift(common, shift_bits), 1)
    signs = 1 - 2 * jnp.bitwise_and(parity, 1)
    return jnp.where(row_index // ROT == col_index // ROT, signs, 0).astype(jnp.bfloat16)


def in_vmem(value):
    return pltpu.with_memory_space_constraint(value, pltpu.VMEM)


def vmem(shape, dtype):
    return pltpu.VMEM(shape, dtype)


def apart_kernel(experts, rows, chunk, n_after, *refs):
    source = refs[0]
    outs = refs[1 + n_after : 1 + n_after + len(experts)]
    done, held, sems = refs[1 + n_after + len(experts) :]
    slots = held.shape[0]
    count = 2 * outs[0].shape[2] // 128
    pieces = [(n, step) for n in range(len(experts)) for step in range(outs[0].shape[1] // rows)]

    def copy(at):
        n, step = pieces[at]
        return pltpu.make_async_copy(
            source.at[experts[n], pl.ds(step * rows * count, rows * count)],
            held.at[at % slots],
            sems.at[at % slots],
        )

    for at in range(min(slots, len(pieces))):
        copy(at).start()
    for at, (n, step) in enumerate(pieces):
        copy(at).wait()
        for row in range(0, rows, chunk):
            pairs = held[at % slots, row * count : (row + chunk) * count, :]
            pairs = jnp.swapaxes(pairs.reshape(chunk, count, 128), 0, 1)
            here = slice(step * rows + row, step * rows + row + chunk)
            for q in range(count):
                outs[n][q % 2, here, (q // 2) * 128 : (q // 2 + 1) * 128] = pairs[q]
        if at + slots < len(pieces):
            copy(at + slots).start()
    done[...] = jnp.zeros_like(done)


def apart(packed, experts, feature_len, inner, after):
    count = 2 * inner // 128
    rows = feature_len // 4 if feature_len % 256 == 0 else feature_len
    chunk = 64 if rows % 64 == 0 else rows
    whole = pl.BlockSpec(memory_space=pltpu.VMEM)
    out = pl.pallas_call(
        functools.partial(apart_kernel, experts, rows, chunk, len(after)),
        in_specs=[pl.BlockSpec(memory_space=pl.ANY)] * (1 + len(after)),
        out_specs=[whole] * (len(experts) + 1),
        out_shape=[vmem((2, feature_len, inner), packed.dtype)] * len(experts)
        + [jax.ShapeDtypeStruct((8, 128), jnp.float32)],
        scratch_shapes=[
            pltpu.VMEM((4, rows * count, 128), packed.dtype),
            pltpu.SemaphoreType.DMA((4,)),
        ],
        compiler_params=pltpu.CompilerParams(vmem_limit_bytes=SMALL_VMEM),
        cost_estimate=pl.CostEstimate(flops=0, bytes_accessed=1024, transcendentals=0),
        name="apart",
    )(packed, *after)
    return out[:-1], out[-1]


def pass_kernel(value, *refs):
    refs[-1][...] = value[...]


def pass_on(value, after):
    return pl.pallas_call(
        pass_kernel,
        in_specs=[pl.BlockSpec(memory_space=pltpu.VMEM)]
        + [pl.BlockSpec(memory_space=pl.ANY)] * len(after),
        out_specs=pl.BlockSpec(memory_space=pltpu.VMEM),
        out_shape=vmem(value.shape, value.dtype),
        compiler_params=pltpu.CompilerParams(vmem_limit_bytes=HIDDEN_VMEM),
        cost_estimate=pl.CostEstimate(flops=0, bytes_accessed=1024, transcendentals=0),
        name="pass_on",
    )(value, *after)


def join_kernel(n_pieces, *refs):
    lanes, out = refs[n_pieces], refs[-1]
    feature_len = refs[0].shape[1]
    base = 0
    for piece in refs[:n_pieces]:
        out[base : base + piece.shape[0], :feature_len] = piece[...]
        base += piece.shape[0]
    out[:, feature_len:] = lanes[...]


def join(pieces, lanes, after):
    whole = pl.BlockSpec(memory_space=pltpu.VMEM)
    return pl.pallas_call(
        functools.partial(join_kernel, len(pieces)),
        in_specs=[whole] * (len(pieces) + 1) + [pl.BlockSpec(memory_space=pl.ANY)] * len(after),
        out_specs=whole,
        out_shape=vmem((lanes.shape[0], pieces[0].shape[1] + lanes.shape[1]), lanes.dtype),
        compiler_params=pltpu.CompilerParams(vmem_limit_bytes=HIDDEN_VMEM),
        cost_estimate=pl.CostEstimate(flops=0, bytes_accessed=1024, transcendentals=0),
        name="join",
    )(*pieces, lanes, *after)


def rotate(sources, signs, target, bases):
    feature_len = target.shape[1]
    width = signs.shape[0]
    for at in range(0, feature_len, width):
        for source, base in zip(sources, bases):
            rotated = jnp.dot(
                source[:, at : at + width], signs[...], preferred_element_type=jnp.float32
            ) * (1.0 / math.sqrt(ROT))
            for piece_at in range(0, width, ROT):
                part = rotated[:, piece_at : piece_at + ROT]
                scale = jnp.max(jnp.abs(part), axis=1, keepdims=True) + 1e-06
                scale = scale.astype(jnp.bfloat16).astype(jnp.float32)
                quantized = (part * (1.0 / scale)).astype(jnp.bfloat16).astype(jnp.float32)
                target[
                    base : base + source.shape[0], at + piece_at : at + piece_at + ROT
                ] = (quantized * scale).astype(jnp.bfloat16)


def first_kernel(n_pieces, *refs):
    signs, out = refs[n_pieces:]
    pieces = refs[:n_pieces]
    rotate(pieces, signs, out, [n * pieces[0].shape[0] for n in range(n_pieces)])


def first_rows(pieces, signs, feature_len):
    whole = pl.BlockSpec(memory_space=pltpu.VMEM)
    rows = sum(piece.shape[0] for piece in pieces)
    return pl.pallas_call(
        functools.partial(first_kernel, len(pieces)),
        in_specs=[whole] * (len(pieces) + 1),
        out_specs=whole,
        out_shape=vmem((rows, feature_len), jnp.bfloat16),
        compiler_params=pltpu.CompilerParams(vmem_limit_bytes=HIDDEN_VMEM),
        cost_estimate=pl.CostEstimate(flops=0, bytes_accessed=1024, transcendentals=0),
        name="first_rows",
    )(*pieces, signs)


def rest_kernel(n_first, n_chips, *refs):
    n_pieces = CORES * n_chips
    index, pieces = refs[0], refs[1 : 1 + n_pieces]
    signs, first, shared, shared_down, *outs, rows_s, sem = refs[1 + n_pieces :]
    deq, shared_hidden, combine, shared_out = outs
    own = shared_out.shape[0]
    own = pl.ds(pl.multiple_of(index[0] * own, own), own)
    copy = pltpu.make_async_copy(shared_down.at[own], shared_out, sem)
    copy.start()
    count = pieces[0].shape[0]
    feature_len = deq.shape[1]
    sources, bases = [], []
    for core in range(CORES):
        for chip in range(n_chips):
            base = (core * n_chips + chip) * count
            if chip == 0:
                piece = pieces[core]
                deq[base : base + count, :] = first[core * count : (core + 1) * count, :]
            else:
                piece = pieces[CORES + core * (n_chips - 1) + chip - 1]
                sources.append(piece)
                bases.append(base)
            rows_s[base : base + count, :] = piece[:, :feature_len]
            combine[base : base + count, :] = piece[:, feature_len:].astype(jnp.float32)
    rotate(sources, signs, deq, bases)
    part = shared.shape[1] // 2
    both = jnp.dot(rows_s[...], shared[...], preferred_element_type=jnp.float32)
    gate, up = both[:, :part], both[:, part:]
    shared_hidden[...] = (gate / (1.0 + jnp.exp(-gate)) * up).astype(jnp.bfloat16)
    copy.wait()


def rest_rows(index, pieces, signs, first, shared, shared_down, n_chips):
    whole = pl.BlockSpec(memory_space=pltpu.VMEM)
    rows = sum(piece.shape[0] for piece in pieces)
    feature_len = first.shape[1]
    return pl.pallas_call(
        functools.partial(rest_kernel, len(pieces), n_chips),
        in_specs=[pl.BlockSpec(memory_space=pltpu.SMEM)]
        + [whole] * (len(pieces) + 3)
        + [pl.BlockSpec(memory_space=pl.ANY)],
        out_specs=[whole] * 4,
        out_shape=[
            vmem((rows, feature_len), jnp.bfloat16),
            vmem((rows, shared.shape[1] // 2), jnp.bfloat16),
            vmem((rows, pieces[0].shape[1] - feature_len), jnp.float32),
            vmem((shared.shape[1] // 2, feature_len), shared_down.dtype),
        ],
        scratch_shapes=[
            pltpu.VMEM((rows, feature_len), jnp.bfloat16),
            pltpu.SemaphoreType.DMA(()),
        ],
        compiler_params=pltpu.CompilerParams(vmem_limit_bytes=HIDDEN_VMEM + 2 * rows * feature_len),
        name="rest_rows",
    )(index, *pieces, signs, first, shared, shared_down)


def hidden_kernel(experts, *refs):
    n = len(experts)
    deq, combine, select, down = refs[:4]
    weights, out = refs[4 : 4 + n], refs[4 + n]
    down_out, sems = refs[5 + n : 5 + 2 * n], refs[5 + 2 * n]
    inner = out.shape[1] // n
    copies = [
        pltpu.make_async_copy(down.at[local], down_out[at], sems.at[at])
        for at, local in enumerate(experts)
    ]
    for copy in copies:
        copy.start()
    for at, local in enumerate(experts):
        gate = jnp.dot(deq[...], weights[at][0], preferred_element_type=jnp.float32)
        up = jnp.dot(deq[...], weights[at][1], preferred_element_type=jnp.float32)
        weight = jnp.sum(combine[...] * select[local : local + 1, :], axis=1, keepdims=True)
        out[:, at * inner : (at + 1) * inner] = (
            gate / (1.0 + jnp.exp(-gate)) * up * weight
        ).astype(jnp.bfloat16)
    for copy in copies:
        copy.wait()


def hidden_rows(deq, combine, select, down, experts, weights):
    whole = pl.BlockSpec(memory_space=pltpu.VMEM)
    rows = deq.shape[0]
    n = len(experts)
    out = pl.pallas_call(
        functools.partial(hidden_kernel, experts),
        in_specs=[whole] * 3 + [pl.BlockSpec(memory_space=pl.ANY)] + [whole] * n,
        out_specs=[whole] * (1 + n),
        out_shape=[
            vmem((rows, n * weights[0].shape[2]), jnp.bfloat16),
            *[vmem(down.shape[1:], down.dtype)] * n,
        ],
        scratch_shapes=[pltpu.SemaphoreType.DMA((n,))],
        compiler_params=pltpu.CompilerParams(vmem_limit_bytes=HIDDEN_VMEM),
        name="hidden_rows",
    )(deq, combine, select, down, *weights)
    return out[0], list(out[1:])


def down_kernel(start, tile, n_hidden, *refs):
    hidden, (shared_hidden, shared_down), downs = (
        refs[:n_hidden],
        refs[n_hidden : n_hidden + 2],
        refs[n_hidden + 2 : -1],
    )
    out = refs[-1]
    inner = downs[0].shape[0]
    per = hidden[0].shape[1] // inner
    for at in range(0, out.shape[1], tile):
        columns = slice(start + at, start + at + tile)
        total = jnp.dot(
            shared_hidden[...], shared_down[:, columns], preferred_element_type=jnp.float32
        )
        for local, down in enumerate(downs):
            units = slice(local % per * inner, (local % per + 1) * inner)
            total += jnp.dot(
                hidden[local // per][:, units],
                down[:, columns],
                preferred_element_type=jnp.float32,
            )
        out[:, at : at + tile] = total.astype(out.dtype)


def down_rows(hidden, shared_hidden, downs, shared_down, start, stop):
    rows = shared_hidden.shape[0]
    tile = math.gcd(256, math.gcd(start, stop - start))
    whole = pl.BlockSpec(memory_space=pltpu.VMEM)
    return pl.pallas_call(
        functools.partial(down_kernel, start, tile, len(hidden)),
        in_specs=[whole] * (2 + len(hidden) + len(downs)),
        out_specs=whole,
        out_shape=vmem((rows, stop - start), jnp.bfloat16),
        compiler_params=pltpu.CompilerParams(vmem_limit_bytes=HIDDEN_VMEM),
        name="down_rows",
    )(*hidden, shared_hidden, shared_down, *downs)


def exchange(value, axis, flip):
    return lax.ppermute(value, axis, [(i, i ^ flip) for i in range(lax.axis_size(axis))])


def per_device(
    tokens,
    expert_ids,
    route_weights,
    pair_flags,
    shared_gate_up,
    shared_down,
    expert_gate_up,
    expert_down,
    readout,
):
    own_rows, feature_len = tokens.shape
    n_local, _, _, inner = expert_gate_up.shape
    expert_count = lax.axis_size("expert")
    narrow_count = lax.axis_size("narrow")
    chips = expert_count // CORES
    experts = n_local * expert_count
    expert_at = lax.axis_index("expert")
    narrow_at = lax.axis_index("narrow")

    named = lax.broadcasted_iota(jnp.int32, (1, 1, experts), 2)
    combine = jnp.sum(
        jnp.where(expert_ids[:, :, None] == named, route_weights[:, :, None], 0.0), axis=1
    )
    high = combine.astype(jnp.bfloat16)
    low = (combine - high.astype(jnp.float32)).astype(jnp.bfloat16)
    columns = -(-2 * experts // 128) * 128
    lanes = jnp.pad(jnp.concatenate([high, low], axis=1), ((0, 0), (0, columns - 2 * experts)))
    lanes = lanes.reshape(narrow_count, own_rows, columns)
    order = narrow_at ^ jnp.arange(narrow_count)
    lanes = lanes[order].reshape(narrow_count * own_rows, columns)
    local_ids = expert_at * n_local + lax.broadcasted_iota(jnp.int32, (n_local, columns), 0)
    column = lax.broadcasted_iota(jnp.int32, (n_local, columns), 1)
    select = ((column == local_ids) | (column == local_ids + experts)).astype(jnp.float32)

    shared_len = shared_down.shape[0]
    part_len = shared_len // expert_count
    if part_len % 128 == 0:
        shared_in = lax.dynamic_slice_in_dim(shared_gate_up, expert_at * part_len, part_len, 2)
        shared_out, index = shared_down, expert_at.reshape(1)
    else:
        mine = lax.broadcasted_iota(jnp.int32, (shared_len, 1), 0) // part_len == expert_at
        shared_in, index = shared_gate_up, jnp.zeros((1,), jnp.int32)
        shared_out = jnp.where(mine, shared_down, jnp.zeros_like(shared_down))
    shared_in = shared_in.reshape(feature_len, -1)
    signs = sign_matrix(2 if feature_len % (2 * ROT) == 0 else 1)

    packed = expert_gate_up.reshape(n_local, feature_len, 2, inner // 128, 128)
    packed = packed.transpose(0, 1, 3, 2, 4).reshape(n_local, -1, 128)
    packed = pltpu.with_memory_space_constraint(packed, pltpu.HBM)

    def prepared(experts, after):
        return apart(packed, experts, feature_len, inner, after)

    early = (n_local + 3) // 4
    from_z = [exchange(tokens, "narrow", flip) for flip in range(1, narrow_count)]
    weights, done = prepared(list(range(early)), [lanes, shared_in, select, signs, index])
    along_z = join([tokens] + from_z, lanes, [done])
    from_x = [exchange(along_z, "expert", flip * CORES) for flip in range(1, chips)]
    near = exchange(along_z, "expert", 1)
    after = [along_z]
    if n_local > early:
        late, done = prepared(list(range(early, n_local)), after)
        weights = weights + late
        after = [done]
    from_x = [pass_on(part, after) for part in from_x]
    from_both = [exchange(part, "expert", 1) for part in from_x]
    first = first_rows([along_z, near], signs, feature_len)

    shared_out = pltpu.with_memory_space_constraint(shared_out, pltpu.HBM)
    deq, shared_hidden, combine, shared_out = rest_rows(
        index, [along_z, near] + from_x + from_both, signs, first, shared_in, shared_out, chips
    )
    down = pltpu.with_memory_space_constraint(expert_down, pltpu.HBM)
    hidden, downs = [], []
    for at in range(0, n_local, 2):
        part, down_part = hidden_rows(
            deq, combine, select, down, list(range(n_local))[at : at + 2], weights[at : at + 2]
        )
        hidden.append(part)
        downs += down_part

    half = own_rows * narrow_count * chips
    cut = feature_len // 256 // 2 * 256

    def by_core(start, stop):
        part = down_rows(hidden, shared_hidden, downs, shared_out, start, stop)
        near = exchange(part[half:], "expert", 1)
        total = part[:half].astype(jnp.float32) + near.astype(jnp.float32)
        return total.reshape(chips, narrow_count, own_rows, stop - start)

    def halve(parts, axis, step):
        pairs = parts.reshape(parts.shape[0] // 2, 2, *parts.shape[1:])
        got = exchange(pairs[:, 1].astype(jnp.bfloat16), axis, step)
        return pairs[:, 0] + got.astype(jnp.float32)

    def add_up(parts, axis, step):
        while parts.shape[0] > 1:
            parts, step = halve(parts, axis, step), 2 * step
        return parts[0]

    totals = []
    if cut:
        parts = halve(jnp.swapaxes(by_core(0, cut), 0, 1), "narrow", 1)
        parts = add_up(jnp.swapaxes(parts, 0, 1), "expert", CORES)
        totals.append(add_up(parts, "narrow", 2))
    totals.append(add_up(add_up(by_core(cut, feature_len), "expert", CORES), "narrow", 1))
    total_sum = jnp.concatenate(totals, axis=1)
    mixed = total_sum.astype(jnp.bfloat16)
    row_score = jnp.sum(total_sum * readout[None, :], axis=1) / jnp.sqrt(
        jnp.mean(total_sum * total_sum, axis=1) + 1e-06
    )
    paired = row_score.reshape(-1, 2)
    pmi_scores = (paired[:, 0] - paired[:, 1]) * (1 - 2 * pair_flags).astype(jnp.float32)
    return (mixed, pmi_scores)


def solution(mesh):
    in_specs = (
        P(("groups", "expert", "narrow"), None),
        P(("groups", "expert"), None),
        P(("groups", "expert"), None),
        P(("groups", "expert", "narrow")),
        P(None, None, "narrow"),
        P("narrow", None),
        P("expert", None, None, "narrow"),
        P("expert", "narrow", None),
        P(),
    )
    out_specs = (P(("groups", "expert", "narrow"), None), P(("groups", "expert", "narrow")))
    return jax.shard_map(
        per_device, mesh=mesh, in_specs=in_specs, out_specs=out_specs, check_vma=False
    )
```

```python
import functools
import math

import jax
import jax.numpy as jnp
from jax import lax
from jax.experimental import pallas as pl
from jax.experimental.pallas import tpu as pltpu
from jax.sharding import PartitionSpec as P

ROT = 128
CORES = 2
SMALL_VMEM = 10 * 1024 * 1024
EARLY = 2
HIDDEN_VMEM = 5 * 1024 * 1024


def sign_matrix(copies):
    size = copies * ROT
    row_index = lax.broadcasted_iota(jnp.int32, (size, size), 0)
    col_index = lax.broadcasted_iota(jnp.int32, (size, size), 1)
    common = jnp.bitwise_and(row_index % ROT, col_index % ROT)
    parity = jnp.zeros((size, size), jnp.int32)
    for shift_bits in range(ROT.bit_length() - 1):
        parity = parity + jnp.bitwise_and(jnp.right_shift(common, shift_bits), 1)
    signs = 1 - 2 * jnp.bitwise_and(parity, 1)
    return jnp.where(row_index // ROT == col_index // ROT, signs, 0).astype(jnp.bfloat16)


def in_vmem(value):
    return pltpu.with_memory_space_constraint(value, pltpu.VMEM)


def vmem(shape, dtype):
    return pltpu.VMEM(shape, dtype)


def apart_kernel(experts, rows, chunk, n_in, *refs):
    source = refs[0]
    outs = refs[n_in : n_in + len(experts)]
    done, *own_out, held, sems = refs[n_in + len(experts) :]
    slots = held.shape[0]
    count = 2 * outs[0].shape[2] // 128
    pieces = [(n, step) for n in range(len(experts)) for step in range(outs[0].shape[1] // rows)]

    def copy(at):
        n, step = pieces[at]
        return pltpu.make_async_copy(
            source.at[experts[n], pl.ds(step * rows * count, rows * count)],
            held.at[at % slots],
            sems.at[at % slots],
        )

    own_copies = []
    for out in own_out:
        columns = pl.ds(refs[1][0] * out.shape[1], out.shape[1])
        own_copies.append(pltpu.make_async_copy(refs[2].at[:, columns], out, sems.at[slots]))
    for at in range(min(slots, len(pieces))):
        copy(at).start()
    for own_copy in own_copies:
        own_copy.start()
    for at, (n, step) in enumerate(pieces):
        copy(at).wait()
        for row in range(0, rows, chunk):
            pairs = held[at % slots, row * count : (row + chunk) * count, :]
            pairs = jnp.swapaxes(pairs.reshape(chunk, count, 128), 0, 1)
            here = slice(step * rows + row, step * rows + row + chunk)
            for q in range(count):
                outs[n][q % 2, here, (q // 2) * 128 : (q // 2 + 1) * 128] = pairs[q]
        if at + slots < len(pieces):
            copy(at + slots).start()
    for own_copy in own_copies:
        own_copy.wait()
    done[...] = jnp.zeros_like(done)


def apart(packed, experts, feature_len, inner, after, shared=None):
    count = 2 * inner // 128
    rows = feature_len // 4 if feature_len % 256 == 0 else feature_len
    chunk = 64 if rows % 64 == 0 else rows
    whole = pl.BlockSpec(memory_space=pltpu.VMEM)
    anywhere = pl.BlockSpec(memory_space=pl.ANY)
    inputs, specs, own = list(after), [anywhere] * len(after), []
    if shared is not None:
        index, columns, units = shared
        inputs = [index, columns] + inputs
        specs = [pl.BlockSpec(memory_space=pltpu.SMEM), anywhere] + specs
        own = [vmem((feature_len, units, 2, 128), columns.dtype)]
    out = pl.pallas_call(
        functools.partial(apart_kernel, experts, rows, chunk, 1 + len(inputs)),
        in_specs=[pl.BlockSpec(memory_space=pl.ANY)] + specs,
        out_specs=[whole] * (len(experts) + 1 + len(own)),
        out_shape=[vmem((2, feature_len, inner), packed.dtype)] * len(experts)
        + [jax.ShapeDtypeStruct((8, 128), jnp.float32)]
        + own,
        scratch_shapes=[
            pltpu.VMEM((4, rows * count, 128), packed.dtype),
            pltpu.SemaphoreType.DMA((5,)),
        ],
        compiler_params=pltpu.CompilerParams(vmem_limit_bytes=SMALL_VMEM),
        cost_estimate=pl.CostEstimate(flops=0, bytes_accessed=1024, transcendentals=0),
        name="apart",
    )(packed, *inputs)
    return out[: len(experts)], out[len(experts)], out[len(experts) + 1 :]


def pass_kernel(value, *refs):
    refs[-1][...] = value[...]


def pass_on(value, after):
    return pl.pallas_call(
        pass_kernel,
        in_specs=[pl.BlockSpec(memory_space=pltpu.VMEM)]
        + [pl.BlockSpec(memory_space=pl.ANY)] * len(after),
        out_specs=pl.BlockSpec(memory_space=pltpu.VMEM),
        out_shape=vmem(value.shape, value.dtype),
        compiler_params=pltpu.CompilerParams(vmem_limit_bytes=HIDDEN_VMEM),
        cost_estimate=pl.CostEstimate(flops=0, bytes_accessed=1024, transcendentals=0),
        name="pass_on",
    )(value, *after)


def join_kernel(n_pieces, *refs):
    lanes, out = refs[n_pieces], refs[-1]
    feature_len = refs[0].shape[1]
    base = 0
    for piece in refs[:n_pieces]:
        out[base : base + piece.shape[0], :feature_len] = piece[...]
        base += piece.shape[0]
    out[:, feature_len:] = lanes[...]


def join(pieces, lanes, after):
    whole = pl.BlockSpec(memory_space=pltpu.VMEM)
    return pl.pallas_call(
        functools.partial(join_kernel, len(pieces)),
        in_specs=[whole] * (len(pieces) + 1) + [pl.BlockSpec(memory_space=pl.ANY)] * len(after),
        out_specs=whole,
        out_shape=vmem((lanes.shape[0], pieces[0].shape[1] + lanes.shape[1]), lanes.dtype),
        compiler_params=pltpu.CompilerParams(vmem_limit_bytes=HIDDEN_VMEM),
        cost_estimate=pl.CostEstimate(flops=0, bytes_accessed=1024, transcendentals=0),
        name="join",
    )(*pieces, lanes, *after)


def rotate(sources, signs, target, bases):
    feature_len = target.shape[1]
    width = signs.shape[0]
    for at in range(0, feature_len, width):
        for source, base in zip(sources, bases):
            rotated = jnp.dot(
                source[:, at : at + width], signs[...], preferred_element_type=jnp.float32
            ) * (1.0 / math.sqrt(ROT))
            for piece_at in range(0, width, ROT):
                part = rotated[:, piece_at : piece_at + ROT]
                scale = jnp.max(jnp.abs(part), axis=1, keepdims=True) + 1e-06
                scale = scale.astype(jnp.bfloat16).astype(jnp.float32)
                quantized = (part * (1.0 / scale)).astype(jnp.bfloat16).astype(jnp.float32)
                target[
                    base : base + source.shape[0], at + piece_at : at + piece_at + ROT
                ] = (quantized * scale).astype(jnp.bfloat16)


def first_kernel(n_pieces, *refs):
    signs, out = refs[n_pieces:]
    pieces = refs[:n_pieces]
    rotate(pieces, signs, out, [n * pieces[0].shape[0] for n in range(n_pieces)])


def first_rows(pieces, signs, feature_len):
    whole = pl.BlockSpec(memory_space=pltpu.VMEM)
    rows = sum(piece.shape[0] for piece in pieces)
    return pl.pallas_call(
        functools.partial(first_kernel, len(pieces)),
        in_specs=[whole] * (len(pieces) + 1),
        out_specs=whole,
        out_shape=vmem((rows, feature_len), jnp.bfloat16),
        compiler_params=pltpu.CompilerParams(vmem_limit_bytes=HIDDEN_VMEM),
        cost_estimate=pl.CostEstimate(flops=0, bytes_accessed=1024, transcendentals=0),
        name="first_rows",
    )(*pieces, signs)


def rest_kernel(n_first, n_chips, *refs):
    n_pieces = CORES * n_chips
    index, pieces = refs[0], refs[1 : 1 + n_pieces]
    signs, first, second, shared, shared_down, *outs, rows_s, sem = refs[1 + n_pieces :]
    deq, shared_hidden, combine, shared_out = outs
    own = shared_out.shape[0]
    own = pl.ds(pl.multiple_of(index[0] * own, own), own)
    copy = pltpu.make_async_copy(shared_down.at[own], shared_out, sem)
    copy.start()
    count = pieces[0].shape[0]
    feature_len = deq.shape[1]
    sources, bases = [], []
    for core in range(CORES):
        for chip in range(n_chips):
            base = (core * n_chips + chip) * count
            if chip == 0:
                piece = pieces[core]
                deq[base : base + count, :] = first[core * count : (core + 1) * count, :]
            else:
                piece = pieces[CORES + core * (n_chips - 1) + chip - 1]
                if core == 0:
                    deq[base : base + count, :] = second[(chip - 1) * count : chip * count, :]
                else:
                    sources.append(piece)
                    bases.append(base)
            rows_s[base : base + count, :] = piece[:, :feature_len]
            combine[base : base + count, :] = piece[:, feature_len:].astype(jnp.float32)
    rotate(sources, signs, deq, bases)
    part = shared.shape[1] // 2
    both = jnp.dot(rows_s[...], shared[...], preferred_element_type=jnp.float32)
    gate, up = both[:, :part], both[:, part:]
    shared_hidden[...] = (gate / (1.0 + jnp.exp(-gate)) * up).astype(jnp.bfloat16)
    copy.wait()


def rest_rows(index, pieces, signs, first, second, shared, shared_down, n_chips):
    whole = pl.BlockSpec(memory_space=pltpu.VMEM)
    rows = sum(piece.shape[0] for piece in pieces)
    feature_len = first.shape[1]
    return pl.pallas_call(
        functools.partial(rest_kernel, len(pieces), n_chips),
        in_specs=[pl.BlockSpec(memory_space=pltpu.SMEM)]
        + [whole] * (len(pieces) + 4)
        + [pl.BlockSpec(memory_space=pl.ANY)],
        out_specs=[whole] * 4,
        out_shape=[
            vmem((rows, feature_len), jnp.bfloat16),
            vmem((rows, shared.shape[1] // 2), jnp.bfloat16),
            vmem((rows, pieces[0].shape[1] - feature_len), jnp.float32),
            vmem((shared.shape[1] // 2, feature_len), shared_down.dtype),
        ],
        scratch_shapes=[
            pltpu.VMEM((rows, feature_len), jnp.bfloat16),
            pltpu.SemaphoreType.DMA(()),
        ],
        compiler_params=pltpu.CompilerParams(vmem_limit_bytes=HIDDEN_VMEM + 2 * rows * feature_len),
        name="rest_rows",
    )(index, *pieces, signs, first, second, shared, shared_down)


def hidden_kernel(experts, *refs):
    n = len(experts)
    deq, combine, select, down = refs[:4]
    weights, out = refs[4 : 4 + n], refs[4 + n]
    down_out, sems = refs[5 + n : 5 + 2 * n], refs[5 + 2 * n]
    inner = out.shape[1] // n
    copies = [
        pltpu.make_async_copy(down.at[local], down_out[at], sems.at[at])
        for at, local in enumerate(experts)
    ]
    for copy in copies:
        copy.start()
    for at, local in enumerate(experts):
        gate = jnp.dot(deq[...], weights[at][0], preferred_element_type=jnp.float32)
        up = jnp.dot(deq[...], weights[at][1], preferred_element_type=jnp.float32)
        weight = jnp.sum(combine[...] * select[local : local + 1, :], axis=1, keepdims=True)
        out[:, at * inner : (at + 1) * inner] = (
            gate / (1.0 + jnp.exp(-gate)) * up * weight
        ).astype(jnp.bfloat16)
    for copy in copies:
        copy.wait()


def hidden_rows(deq, combine, select, down, experts, weights):
    whole = pl.BlockSpec(memory_space=pltpu.VMEM)
    rows = deq.shape[0]
    n = len(experts)
    out = pl.pallas_call(
        functools.partial(hidden_kernel, experts),
        in_specs=[whole] * 3 + [pl.BlockSpec(memory_space=pl.ANY)] + [whole] * n,
        out_specs=[whole] * (1 + n),
        out_shape=[
            vmem((rows, n * weights[0].shape[2]), jnp.bfloat16),
            *[vmem(down.shape[1:], down.dtype)] * n,
        ],
        scratch_shapes=[pltpu.SemaphoreType.DMA((n,))],
        compiler_params=pltpu.CompilerParams(vmem_limit_bytes=HIDDEN_VMEM),
        name="hidden_rows",
    )(deq, combine, select, down, *weights)
    return out[0], list(out[1:])


def down_kernel(start, tile, n_hidden, *refs):
    hidden, (shared_hidden, shared_down), downs = (
        refs[:n_hidden],
        refs[n_hidden : n_hidden + 2],
        refs[n_hidden + 2 : -1],
    )
    out = refs[-1]
    inner = downs[0].shape[0]
    per = hidden[0].shape[1] // inner
    for at in range(0, out.shape[1], tile):
        columns = slice(start + at, start + at + tile)
        total = jnp.dot(
            shared_hidden[...], shared_down[:, columns], preferred_element_type=jnp.float32
        )
        for local, down in enumerate(downs):
            units = slice(local % per * inner, (local % per + 1) * inner)
            total += jnp.dot(
                hidden[local // per][:, units],
                down[:, columns],
                preferred_element_type=jnp.float32,
            )
        out[:, at : at + tile] = total.astype(out.dtype)


def down_rows(hidden, shared_hidden, downs, shared_down, start, stop):
    rows = shared_hidden.shape[0]
    tile = math.gcd(256, math.gcd(start, stop - start))
    whole = pl.BlockSpec(memory_space=pltpu.VMEM)
    return pl.pallas_call(
        functools.partial(down_kernel, start, tile, len(hidden)),
        in_specs=[whole] * (2 + len(hidden) + len(downs)),
        out_specs=whole,
        out_shape=vmem((rows, stop - start), jnp.bfloat16),
        compiler_params=pltpu.CompilerParams(vmem_limit_bytes=HIDDEN_VMEM),
        name="down_rows",
    )(*hidden, shared_hidden, shared_down, *downs)


def finish_kernel(n_parts, *refs):
    parts = refs[: 2 * n_parts]
    readout, flags, mixed, scores = refs[2 * n_parts :]
    rows, feature_len = mixed.shape
    pairs = scores.shape[1]
    at = 0
    dots = jnp.zeros((rows, 1), jnp.float32)
    squares = jnp.zeros((rows, 1), jnp.float32)
    for part, got in zip(parts[::2], parts[1::2]):
        total = part[...] + got[...].astype(jnp.float32)
        columns = slice(at, at + total.shape[1])
        mixed[:, columns] = total.astype(mixed.dtype)
        dots += jnp.sum(total * readout[:, columns], axis=1, keepdims=True)
        squares += jnp.sum(total * total, axis=1, keepdims=True)
        at += total.shape[1]
    row_score = dots / jnp.sqrt(squares * (1.0 / feature_len) + 1e-06)
    row = lax.broadcasted_iota(jnp.int32, (rows, pairs), 0)
    first = 2 * lax.broadcasted_iota(jnp.int32, (rows, pairs), 1)
    signed = jnp.where(row == first, row_score, jnp.where(row == first + 1, -row_score, 0.0))
    scores[...] = jnp.sum(signed, axis=0, keepdims=True) * (1 - 2 * flags[...]).astype(jnp.float32)


def finish(parts, readout, pair_flags):
    whole = pl.BlockSpec(memory_space=pltpu.VMEM)
    rows = parts[0][0].shape[0]
    flat = [term for part in parts for term in part]
    mixed, scores = pl.pallas_call(
        functools.partial(finish_kernel, len(parts)),
        in_specs=[whole] * (len(flat) + 2),
        out_specs=[whole] * 2,
        out_shape=[
            jax.ShapeDtypeStruct((rows, readout.shape[0]), jnp.bfloat16),
            jax.ShapeDtypeStruct((1, rows // 2), jnp.float32),
        ],
        compiler_params=pltpu.CompilerParams(vmem_limit_bytes=HIDDEN_VMEM),
        name="finish",
    )(*flat, readout.reshape(1, -1), pair_flags.reshape(1, -1))
    return mixed, scores.reshape(-1)


def exchange(value, axis, flip):
    return lax.ppermute(value, axis, [(i, i ^ flip) for i in range(lax.axis_size(axis))])


def per_device(
    tokens,
    expert_ids,
    route_weights,
    pair_flags,
    shared_gate_up,
    shared_down,
    expert_gate_up,
    expert_down,
    readout,
):
    own_rows, feature_len = tokens.shape
    n_local, _, _, inner = expert_gate_up.shape
    expert_count = lax.axis_size("expert")
    narrow_count = lax.axis_size("narrow")
    chips = expert_count // CORES
    experts = n_local * expert_count
    expert_at = lax.axis_index("expert")
    narrow_at = lax.axis_index("narrow")

    named = lax.broadcasted_iota(jnp.int32, (1, 1, experts), 2)
    combine = jnp.sum(
        jnp.where(expert_ids[:, :, None] == named, route_weights[:, :, None], 0.0), axis=1
    )
    high = combine.astype(jnp.bfloat16)
    low = (combine - high.astype(jnp.float32)).astype(jnp.bfloat16)
    columns = -(-2 * experts // 128) * 128
    lanes = jnp.pad(jnp.concatenate([high, low], axis=1), ((0, 0), (0, columns - 2 * experts)))
    lanes = lanes.reshape(narrow_count, own_rows, columns)
    order = narrow_at ^ jnp.arange(narrow_count)
    lanes = lanes[order].reshape(narrow_count * own_rows, columns)
    local_ids = expert_at * n_local + lax.broadcasted_iota(jnp.int32, (n_local, columns), 0)
    column = lax.broadcasted_iota(jnp.int32, (n_local, columns), 1)
    select = ((column == local_ids) | (column == local_ids + experts)).astype(jnp.float32)

    shared_len = shared_down.shape[0]
    part_len = shared_len // expert_count
    if part_len % 128 == 0:
        shared_out, index = shared_down, expert_at.reshape(1)
        columns_of = shared_gate_up.reshape(feature_len, 2, shared_len // 128, 128)
        columns_of = pltpu.with_memory_space_constraint(
            columns_of.transpose(0, 2, 1, 3), pltpu.HBM
        )
        shared = (index, columns_of, part_len // 128)
    else:
        mine = lax.broadcasted_iota(jnp.int32, (shared_len, 1), 0) // part_len == expert_at
        shared_in, index = shared_gate_up.reshape(feature_len, -1), jnp.zeros((1,), jnp.int32)
        shared_out = jnp.where(mine, shared_down, jnp.zeros_like(shared_down))
        shared = None
    signs = sign_matrix(2 if feature_len % (2 * ROT) == 0 else 1)

    packed = expert_gate_up.reshape(n_local, feature_len, 2, inner // 128, 128)
    packed = packed.transpose(0, 1, 3, 2, 4).reshape(n_local, -1, 128)
    packed = pltpu.with_memory_space_constraint(packed, pltpu.HBM)

    early = (n_local + EARLY - 1) // EARLY
    from_z = [exchange(tokens, "narrow", flip) for flip in range(1, narrow_count)]
    weights, done, own = apart(
        packed, [0], feature_len, inner, [lanes, select, signs, index], shared
    )
    for expert in range(1, early):
        more, done, _ = apart(packed, [expert], feature_len, inner, [done])
        weights = weights + more
    if own:
        shared_in = own[0].transpose(0, 2, 1, 3).reshape(feature_len, -1)
    along_z = join([tokens] + from_z, lanes, [done])
    from_x = [exchange(along_z, "expert", flip * CORES) for flip in range(1, chips)]
    near = exchange(along_z, "expert", 1)
    after = [along_z]
    if n_local > early:
        late, done, _ = apart(
            packed, list(range(early, n_local)), feature_len, inner, after + [shared_in]
        )
        weights = weights + late
        after = [done]
    first = first_rows([along_z, near], signs, feature_len)
    from_x = [pass_on(part, after + [first]) for part in from_x]
    from_both = [exchange(part, "expert", 1) for part in from_x]
    second = first_rows(from_x, signs, feature_len)

    shared_out = pltpu.with_memory_space_constraint(shared_out, pltpu.HBM)
    deq, shared_hidden, combine, shared_out = rest_rows(
        index,
        [along_z, near] + from_x + from_both,
        signs,
        first,
        second,
        shared_in,
        shared_out,
        chips,
    )
    down = pltpu.with_memory_space_constraint(expert_down, pltpu.HBM)
    hidden, downs = [], []
    for at in range(0, n_local, 2):
        part, down_part = hidden_rows(
            deq, combine, select, down, list(range(n_local))[at : at + 2], weights[at : at + 2]
        )
        hidden.append(part)
        downs += down_part

    half = own_rows * narrow_count * chips
    cut = feature_len // 256 // 2 * 256

    def by_core(start, stop):
        part = down_rows(hidden, shared_hidden, downs, shared_out, start, stop)
        near = exchange(part[half:], "expert", 1)
        total = part[:half].astype(jnp.float32) + near.astype(jnp.float32)
        return total.reshape(chips, narrow_count, own_rows, stop - start)

    def halve(parts, axis, step):
        pairs = parts.reshape(parts.shape[0] // 2, 2, *parts.shape[1:])
        got = exchange(pairs[:, 1].astype(jnp.bfloat16), axis, step)
        return pairs[:, 0] + got.astype(jnp.float32)

    def add_up(parts, axis, step):
        while parts.shape[0] > 1:
            parts, step = halve(parts, axis, step), 2 * step
        return parts[0]

    def last_pair(parts, step):
        while parts.shape[0] > 2:
            parts, step = halve(parts, "narrow", step), 2 * step
        return parts[0], exchange(parts[1].astype(jnp.bfloat16), "narrow", step)

    parts = halve(jnp.swapaxes(by_core(0, cut), 0, 1), "narrow", 1)
    parts = add_up(jnp.swapaxes(parts, 0, 1), "expert", CORES)
    left = last_pair(parts, 2)
    right = last_pair(add_up(by_core(cut, feature_len), "expert", CORES), 1)
    return finish([left, right], readout, pair_flags)


def solution(mesh):
    in_specs = (
        P(("groups", "expert", "narrow"), None),
        P(("groups", "expert"), None),
        P(("groups", "expert"), None),
        P(("groups", "expert", "narrow")),
        P(None, None, "narrow"),
        P("narrow", None),
        P("expert", None, None, "narrow"),
        P("expert", "narrow", None),
        P(),
    )
    out_specs = (P(("groups", "expert", "narrow"), None), P(("groups", "expert", "narrow")))
    return jax.shard_map(
        per_device, mesh=mesh, in_specs=in_specs, out_specs=out_specs, check_vma=False
    )
```

```python
import functools
import math

import jax
import jax.numpy as jnp
from jax import lax
from jax.experimental import pallas as pl
from jax.experimental.pallas import tpu as pltpu
from jax.sharding import PartitionSpec as P

ROT = 128
CORES = 2
SMALL_VMEM = 10 * 1024 * 1024
EARLY = 4
HIDDEN_VMEM = 5 * 1024 * 1024


def sign_matrix(copies):
    size = copies * ROT
    row_index = lax.broadcasted_iota(jnp.int32, (size, size), 0)
    col_index = lax.broadcasted_iota(jnp.int32, (size, size), 1)
    common = jnp.bitwise_and(row_index % ROT, col_index % ROT)
    parity = jnp.zeros((size, size), jnp.int32)
    for shift_bits in range(ROT.bit_length() - 1):
        parity = parity + jnp.bitwise_and(jnp.right_shift(common, shift_bits), 1)
    signs = 1 - 2 * jnp.bitwise_and(parity, 1)
    return jnp.where(row_index // ROT == col_index // ROT, signs, 0).astype(jnp.bfloat16)


def in_vmem(value):
    return pltpu.with_memory_space_constraint(value, pltpu.VMEM)


def vmem(shape, dtype):
    return pltpu.VMEM(shape, dtype)


def apart_kernel(experts, rows, chunk, n_in, *refs):
    source = refs[0]
    outs = refs[n_in : n_in + len(experts)]
    done, *own_out, held, sems = refs[n_in + len(experts) :]
    slots = held.shape[0]
    count = 2 * outs[0].shape[2] // 128
    pieces = [(n, step) for n in range(len(experts)) for step in range(outs[0].shape[1] // rows)]

    def copy(at):
        n, step = pieces[at]
        return pltpu.make_async_copy(
            source.at[experts[n], pl.ds(step * rows * count, rows * count)],
            held.at[at % slots],
            sems.at[at % slots],
        )

    own_copies = []
    for out in own_out:
        columns = pl.ds(refs[1][0] * out.shape[1], out.shape[1])
        own_copies.append(pltpu.make_async_copy(refs[2].at[:, columns], out, sems.at[slots]))
    for at in range(min(slots, len(pieces))):
        copy(at).start()
    for own_copy in own_copies:
        own_copy.start()
    for at, (n, step) in enumerate(pieces):
        copy(at).wait()
        for row in range(0, rows, chunk):
            pairs = held[at % slots, row * count : (row + chunk) * count, :]
            pairs = jnp.swapaxes(pairs.reshape(chunk, count, 128), 0, 1)
            here = slice(step * rows + row, step * rows + row + chunk)
            for q in range(count):
                outs[n][q % 2, here, (q // 2) * 128 : (q // 2 + 1) * 128] = pairs[q]
        if at + slots < len(pieces):
            copy(at + slots).start()
    for own_copy in own_copies:
        own_copy.wait()
    done[...] = jnp.zeros_like(done)


def apart(packed, experts, feature_len, inner, after, shared=None):
    count = 2 * inner // 128
    rows = feature_len // 4 if feature_len % 256 == 0 else feature_len
    chunk = 64 if rows % 64 == 0 else rows
    whole = pl.BlockSpec(memory_space=pltpu.VMEM)
    anywhere = pl.BlockSpec(memory_space=pl.ANY)
    inputs, specs, own = list(after), [anywhere] * len(after), []
    if shared is not None:
        index, columns, units = shared
        inputs = [index, columns] + inputs
        specs = [pl.BlockSpec(memory_space=pltpu.SMEM), anywhere] + specs
        own = [vmem((feature_len, units, 2, 128), columns.dtype)]
    out = pl.pallas_call(
        functools.partial(apart_kernel, experts, rows, chunk, 1 + len(inputs)),
        in_specs=[pl.BlockSpec(memory_space=pl.ANY)] + specs,
        out_specs=[whole] * (len(experts) + 1 + len(own)),
        out_shape=[vmem((2, feature_len, inner), packed.dtype)] * len(experts)
        + [jax.ShapeDtypeStruct((8, 128), jnp.float32)]
        + own,
        scratch_shapes=[
            pltpu.VMEM((4, rows * count, 128), packed.dtype),
            pltpu.SemaphoreType.DMA((5,)),
        ],
        compiler_params=pltpu.CompilerParams(vmem_limit_bytes=SMALL_VMEM),
        cost_estimate=pl.CostEstimate(flops=0, bytes_accessed=1024, transcendentals=0),
        name="apart",
    )(packed, *inputs)
    return out[: len(experts)], out[len(experts)], out[len(experts) + 1 :]


def pass_kernel(n_pieces, *refs):
    out = refs[-1]
    base = 0
    for piece in refs[:n_pieces]:
        out[base : base + piece.shape[0], :] = piece[...]
        base += piece.shape[0]


def pass_on(pieces, after):
    rows = sum(piece.shape[0] for piece in pieces)
    return pl.pallas_call(
        functools.partial(pass_kernel, len(pieces)),
        in_specs=[pl.BlockSpec(memory_space=pltpu.VMEM)] * len(pieces)
        + [pl.BlockSpec(memory_space=pl.ANY)] * len(after),
        out_specs=pl.BlockSpec(memory_space=pltpu.VMEM),
        out_shape=vmem((rows, pieces[0].shape[1]), pieces[0].dtype),
        compiler_params=pltpu.CompilerParams(vmem_limit_bytes=HIDDEN_VMEM),
        cost_estimate=pl.CostEstimate(flops=0, bytes_accessed=1024, transcendentals=0),
        name="pass_on",
    )(*pieces, *after)


def pack_kernel(rows, lanes, out):
    out[:, : rows.shape[1]] = rows[...]
    out[:, rows.shape[1] :] = lanes[...]


def pack(rows, lanes):
    whole = pl.BlockSpec(memory_space=pltpu.VMEM)
    return pl.pallas_call(
        pack_kernel,
        in_specs=[whole] * 2,
        out_specs=whole,
        out_shape=vmem((rows.shape[0], rows.shape[1] + lanes.shape[1]), rows.dtype),
        compiler_params=pltpu.CompilerParams(vmem_limit_bytes=HIDDEN_VMEM),
        cost_estimate=pl.CostEstimate(flops=0, bytes_accessed=1024, transcendentals=0),
        name="pack",
    )(rows, lanes)


def join_kernel(n_pieces, *refs):
    lanes, out, others = refs[n_pieces], refs[-2], refs[-1]
    feature_len = refs[0].shape[1]
    own = out.shape[0] - others.shape[0]
    base = 0
    for piece in refs[:n_pieces]:
        out[base : base + piece.shape[0], :feature_len] = piece[...]
        if base:
            others[base - own : base - own + piece.shape[0], :feature_len] = piece[...]
        base += piece.shape[0]
    out[:, feature_len:] = lanes[...]
    others[:, feature_len:] = lanes[own:, :]


def join(pieces, lanes, after):
    whole = pl.BlockSpec(memory_space=pltpu.VMEM)
    rows, own = lanes.shape[0], pieces[0].shape[0]
    columns = pieces[0].shape[1] + lanes.shape[1]
    return pl.pallas_call(
        functools.partial(join_kernel, len(pieces)),
        in_specs=[whole] * (len(pieces) + 1) + [pl.BlockSpec(memory_space=pl.ANY)] * len(after),
        out_specs=[whole] * 2,
        out_shape=[vmem((rows, columns), lanes.dtype), vmem((rows - own, columns), lanes.dtype)],
        compiler_params=pltpu.CompilerParams(vmem_limit_bytes=HIDDEN_VMEM),
        cost_estimate=pl.CostEstimate(flops=0, bytes_accessed=1024, transcendentals=0),
        name="join",
    )(*pieces, lanes, *after)


def rotate(sources, signs, target, bases):
    feature_len = target.shape[1]
    width = signs.shape[0]
    for at in range(0, feature_len, width):
        for source, base in zip(sources, bases):
            rotated = jnp.dot(
                source[:, at : at + width], signs[...], preferred_element_type=jnp.float32
            ) * (1.0 / math.sqrt(ROT))
            for piece_at in range(0, width, ROT):
                part = rotated[:, piece_at : piece_at + ROT]
                scale = jnp.max(jnp.abs(part), axis=1, keepdims=True) + 1e-06
                scale = scale.astype(jnp.bfloat16).astype(jnp.float32)
                quantized = (part * (1.0 / scale)).astype(jnp.bfloat16).astype(jnp.float32)
                target[
                    base : base + source.shape[0], at + piece_at : at + piece_at + ROT
                ] = (quantized * scale).astype(jnp.bfloat16)


def first_kernel(n_pieces, *refs):
    signs, out = refs[n_pieces:]
    pieces = refs[:n_pieces]
    rotate(pieces, signs, out, [n * pieces[0].shape[0] for n in range(n_pieces)])


def first_rows(pieces, signs, feature_len):
    whole = pl.BlockSpec(memory_space=pltpu.VMEM)
    rows = sum(piece.shape[0] for piece in pieces)
    return pl.pallas_call(
        functools.partial(first_kernel, len(pieces)),
        in_specs=[whole] * (len(pieces) + 1),
        out_specs=whole,
        out_shape=vmem((rows, feature_len), jnp.bfloat16),
        compiler_params=pltpu.CompilerParams(vmem_limit_bytes=HIDDEN_VMEM),
        cost_estimate=pl.CostEstimate(flops=0, bytes_accessed=1024, transcendentals=0),
        name="first_rows",
    )(*pieces, signs)


def rest_kernel(n_first, n_chips, *refs):
    n_pieces = CORES * n_chips
    index, pieces = refs[0], refs[1 : 1 + n_pieces]
    signs, first, second, shared, shared_down, *outs, rows_s, sem = refs[1 + n_pieces :]
    deq, shared_hidden, combine, shared_out = outs
    own = shared_out.shape[0]
    own = pl.ds(pl.multiple_of(index[0] * own, own), own)
    copy = pltpu.make_async_copy(shared_down.at[own], shared_out, sem)
    copy.start()
    count = pieces[0].shape[0]
    feature_len = deq.shape[1]
    sources, bases = [], []
    for core in range(CORES):
        for chip in range(n_chips):
            base = (core * n_chips + chip) * count
            if chip == 0:
                piece = pieces[core]
                deq[base : base + count, :] = first[core * count : (core + 1) * count, :]
            else:
                piece = pieces[CORES + core * (n_chips - 1) + chip - 1]
                if core == 0:
                    deq[base : base + count, :] = second[(chip - 1) * count : chip * count, :]
                else:
                    sources.append(piece)
                    bases.append(base)
            rows_s[base : base + count, :] = piece[:, :feature_len]
            combine[base : base + count, :] = piece[:, feature_len:].astype(jnp.float32)
    rotate(sources, signs, deq, bases)
    part = shared.shape[1] // 2
    both = jnp.dot(rows_s[...], shared[...], preferred_element_type=jnp.float32)
    gate, up = both[:, :part], both[:, part:]
    shared_hidden[...] = (gate / (1.0 + jnp.exp(-gate)) * up).astype(jnp.bfloat16)
    copy.wait()


def rest_rows(index, pieces, signs, first, second, shared, shared_down, n_chips):
    whole = pl.BlockSpec(memory_space=pltpu.VMEM)
    rows = sum(piece.shape[0] for piece in pieces)
    feature_len = first.shape[1]
    return pl.pallas_call(
        functools.partial(rest_kernel, len(pieces), n_chips),
        in_specs=[pl.BlockSpec(memory_space=pltpu.SMEM)]
        + [whole] * (len(pieces) + 4)
        + [pl.BlockSpec(memory_space=pl.ANY)],
        out_specs=[whole] * 4,
        out_shape=[
            vmem((rows, feature_len), jnp.bfloat16),
            vmem((rows, shared.shape[1] // 2), jnp.bfloat16),
            vmem((rows, pieces[0].shape[1] - feature_len), jnp.float32),
            vmem((shared.shape[1] // 2, feature_len), shared_down.dtype),
        ],
        scratch_shapes=[
            pltpu.VMEM((rows, feature_len), jnp.bfloat16),
            pltpu.SemaphoreType.DMA(()),
        ],
        compiler_params=pltpu.CompilerParams(vmem_limit_bytes=HIDDEN_VMEM + 2 * rows * feature_len),
        name="rest_rows",
    )(index, *pieces, signs, first, second, shared, shared_down)


def hidden_kernel(experts, *refs):
    n = len(experts)
    deq, combine, select, down = refs[:4]
    weights, out = refs[4 : 4 + n], refs[4 + n]
    down_out, sems = refs[5 + n : 5 + 2 * n], refs[5 + 2 * n]
    inner = out.shape[1] // n
    copies = [
        pltpu.make_async_copy(down.at[local], down_out[at], sems.at[at])
        for at, local in enumerate(experts)
    ]
    for copy in copies:
        copy.start()
    for at, local in enumerate(experts):
        gate = jnp.dot(deq[...], weights[at][0], preferred_element_type=jnp.float32)
        up = jnp.dot(deq[...], weights[at][1], preferred_element_type=jnp.float32)
        weight = jnp.sum(combine[...] * select[local : local + 1, :], axis=1, keepdims=True)
        out[:, at * inner : (at + 1) * inner] = (
            gate / (1.0 + jnp.exp(-gate)) * up * weight
        ).astype(jnp.bfloat16)
    for copy in copies:
        copy.wait()


def hidden_rows(deq, combine, select, down, experts, weights):
    whole = pl.BlockSpec(memory_space=pltpu.VMEM)
    rows = deq.shape[0]
    n = len(experts)
    out = pl.pallas_call(
        functools.partial(hidden_kernel, experts),
        in_specs=[whole] * 3 + [pl.BlockSpec(memory_space=pl.ANY)] + [whole] * n,
        out_specs=[whole] * (1 + n),
        out_shape=[
            vmem((rows, n * weights[0].shape[2]), jnp.bfloat16),
            *[vmem(down.shape[1:], down.dtype)] * n,
        ],
        scratch_shapes=[pltpu.SemaphoreType.DMA((n,))],
        compiler_params=pltpu.CompilerParams(vmem_limit_bytes=HIDDEN_VMEM),
        name="hidden_rows",
    )(deq, combine, select, down, *weights)
    return out[0], list(out[1:])


def down_kernel(start, tile, n_hidden, *refs):
    hidden, (shared_hidden, shared_down), downs = (
        refs[:n_hidden],
        refs[n_hidden : n_hidden + 2],
        refs[n_hidden + 2 : -1],
    )
    out = refs[-1]
    inner = downs[0].shape[0]
    per = hidden[0].shape[1] // inner
    for at in range(0, out.shape[1], tile):
        columns = slice(start + at, start + at + tile)
        total = jnp.dot(
            shared_hidden[...], shared_down[:, columns], preferred_element_type=jnp.float32
        )
        for local, down in enumerate(downs):
            units = slice(local % per * inner, (local % per + 1) * inner)
            total += jnp.dot(
                hidden[local // per][:, units],
                down[:, columns],
                preferred_element_type=jnp.float32,
            )
        out[:, at : at + tile] = total.astype(out.dtype)


def down_rows(hidden, shared_hidden, downs, shared_down, start, stop):
    rows = shared_hidden.shape[0]
    tile = math.gcd(256, math.gcd(start, stop - start))
    whole = pl.BlockSpec(memory_space=pltpu.VMEM)
    return pl.pallas_call(
        functools.partial(down_kernel, start, tile, len(hidden)),
        in_specs=[whole] * (2 + len(hidden) + len(downs)),
        out_specs=whole,
        out_shape=vmem((rows, stop - start), jnp.bfloat16),
        compiler_params=pltpu.CompilerParams(vmem_limit_bytes=HIDDEN_VMEM),
        name="down_rows",
    )(*hidden, shared_hidden, shared_down, *downs)


def finish_kernel(n_parts, *refs):
    parts = refs[: 2 * n_parts]
    readout, flags, mixed, scores = refs[2 * n_parts :]
    rows, feature_len = mixed.shape
    pairs = scores.shape[1]
    at = 0
    dots = jnp.zeros((rows, 1), jnp.float32)
    squares = jnp.zeros((rows, 1), jnp.float32)
    for part, got in zip(parts[::2], parts[1::2]):
        total = part[...] + got[...].astype(jnp.float32)
        columns = slice(at, at + total.shape[1])
        mixed[:, columns] = total.astype(mixed.dtype)
        dots += jnp.sum(total * readout[:, columns], axis=1, keepdims=True)
        squares += jnp.sum(total * total, axis=1, keepdims=True)
        at += total.shape[1]
    row_score = dots / jnp.sqrt(squares * (1.0 / feature_len) + 1e-06)
    row = lax.broadcasted_iota(jnp.int32, (rows, pairs), 0)
    first = 2 * lax.broadcasted_iota(jnp.int32, (rows, pairs), 1)
    signed = jnp.where(row == first, row_score, jnp.where(row == first + 1, -row_score, 0.0))
    scores[...] = jnp.sum(signed, axis=0, keepdims=True) * (1 - 2 * flags[...]).astype(jnp.float32)


def finish(parts, readout, pair_flags):
    whole = pl.BlockSpec(memory_space=pltpu.VMEM)
    rows = parts[0][0].shape[0]
    flat = [term for part in parts for term in part]
    mixed, scores = pl.pallas_call(
        functools.partial(finish_kernel, len(parts)),
        in_specs=[whole] * (len(flat) + 2),
        out_specs=[whole] * 2,
        out_shape=[
            jax.ShapeDtypeStruct((rows, readout.shape[0]), jnp.bfloat16),
            jax.ShapeDtypeStruct((1, rows // 2), jnp.float32),
        ],
        compiler_params=pltpu.CompilerParams(vmem_limit_bytes=HIDDEN_VMEM),
        name="finish",
    )(*flat, readout.reshape(1, -1), pair_flags.reshape(1, -1))
    return mixed, scores.reshape(-1)


def exchange(value, axis, flip):
    return lax.ppermute(value, axis, [(i, i ^ flip) for i in range(lax.axis_size(axis))])


def per_device(
    tokens,
    expert_ids,
    route_weights,
    pair_flags,
    shared_gate_up,
    shared_down,
    expert_gate_up,
    expert_down,
    readout,
):
    own_rows, feature_len = tokens.shape
    n_local, _, _, inner = expert_gate_up.shape
    expert_count = lax.axis_size("expert")
    narrow_count = lax.axis_size("narrow")
    chips = expert_count // CORES
    experts = n_local * expert_count
    expert_at = lax.axis_index("expert")
    narrow_at = lax.axis_index("narrow")

    named = lax.broadcasted_iota(jnp.int32, (1, 1, experts), 2)
    combine = jnp.sum(
        jnp.where(expert_ids[:, :, None] == named, route_weights[:, :, None], 0.0), axis=1
    )
    high = combine.astype(jnp.bfloat16)
    low = (combine - high.astype(jnp.float32)).astype(jnp.bfloat16)
    columns = -(-2 * experts // 128) * 128
    lanes = jnp.pad(jnp.concatenate([high, low], axis=1), ((0, 0), (0, columns - 2 * experts)))
    lanes = lanes.reshape(narrow_count, own_rows, columns)
    order = narrow_at ^ jnp.arange(narrow_count)
    lanes = lanes[order].reshape(narrow_count * own_rows, columns)
    local_ids = expert_at * n_local + lax.broadcasted_iota(jnp.int32, (n_local, columns), 0)
    column = lax.broadcasted_iota(jnp.int32, (n_local, columns), 1)
    select = ((column == local_ids) | (column == local_ids + experts)).astype(jnp.float32)

    shared_len = shared_down.shape[0]
    part_len = shared_len // expert_count
    if part_len % 128 == 0:
        shared_out, index = shared_down, expert_at.reshape(1)
        columns_of = shared_gate_up.reshape(feature_len, 2, shared_len // 128, 128)
        columns_of = pltpu.with_memory_space_constraint(
            columns_of.transpose(0, 2, 1, 3), pltpu.HBM
        )
        shared = (index, columns_of, part_len // 128)
    else:
        mine = lax.broadcasted_iota(jnp.int32, (shared_len, 1), 0) // part_len == expert_at
        shared_in, index = shared_gate_up.reshape(feature_len, -1), jnp.zeros((1,), jnp.int32)
        shared_out = jnp.where(mine, shared_down, jnp.zeros_like(shared_down))
        shared = None
    signs = sign_matrix(2 if feature_len % (2 * ROT) == 0 else 1)

    packed = expert_gate_up.reshape(n_local, feature_len, 2, inner // 128, 128)
    packed = packed.transpose(0, 1, 3, 2, 4).reshape(n_local, -1, 128)
    packed = pltpu.with_memory_space_constraint(packed, pltpu.HBM)

    early = (n_local + EARLY - 1) // EARLY
    from_z = [exchange(tokens, "narrow", flip) for flip in range(1, narrow_count)]
    packed_own = pack(tokens, lanes[:own_rows])
    own_from_x = [exchange(packed_own, "expert", flip * CORES) for flip in range(1, chips)]
    weights, done, own = apart(
        packed, [0], feature_len, inner, [lanes, select, signs, index, packed_own], shared
    )
    for expert in range(1, early):
        more, done, _ = apart(packed, [expert], feature_len, inner, [done])
        weights = weights + more
    if own:
        shared_in = own[0].transpose(0, 2, 1, 3).reshape(feature_len, -1)
    along_z, others = join([tokens] + from_z, lanes, [done] + own_from_x)
    from_x = [exchange(others, "expert", flip * CORES) for flip in range(1, chips)]
    near = exchange(along_z, "expert", 1)
    after = [along_z]
    if n_local > early:
        late, done, _ = apart(
            packed, list(range(early, n_local)), feature_len, inner, after + [shared_in]
        )
        weights = weights + late
        after = [done]
    first = first_rows([along_z, near], signs, feature_len)
    from_x = [pass_on([own, part], after + [first]) for own, part in zip(own_from_x, from_x)]
    from_both = [exchange(part, "expert", 1) for part in from_x]
    second = first_rows(from_x, signs, feature_len)

    shared_out = pltpu.with_memory_space_constraint(shared_out, pltpu.HBM)
    deq, shared_hidden, combine, shared_out = rest_rows(
        index,
        [along_z, near] + from_x + from_both,
        signs,
        first,
        second,
        shared_in,
        shared_out,
        chips,
    )
    down = pltpu.with_memory_space_constraint(expert_down, pltpu.HBM)
    hidden, downs = [], []
    for at in range(0, n_local, 2):
        part, down_part = hidden_rows(
            deq, combine, select, down, list(range(n_local))[at : at + 2], weights[at : at + 2]
        )
        hidden.append(part)
        downs += down_part

    half = own_rows * narrow_count * chips
    cut = feature_len // 256 // 2 * 256

    def by_core(start, stop):
        part = down_rows(hidden, shared_hidden, downs, shared_out, start, stop)
        near = exchange(part[half:], "expert", 1)
        total = part[:half].astype(jnp.float32) + near.astype(jnp.float32)
        return total.reshape(chips, narrow_count, own_rows, stop - start)

    def halve(parts, axis, step):
        pairs = parts.reshape(parts.shape[0] // 2, 2, *parts.shape[1:])
        got = exchange(pairs[:, 1].astype(jnp.bfloat16), axis, step)
        return pairs[:, 0] + got.astype(jnp.float32)

    def add_up(parts, axis, step):
        while parts.shape[0] > 1:
            parts, step = halve(parts, axis, step), 2 * step
        return parts[0]

    def last_pair(parts, step):
        while parts.shape[0] > 2:
            parts, step = halve(parts, "narrow", step), 2 * step
        return parts[0], exchange(parts[1].astype(jnp.bfloat16), "narrow", step)

    parts = halve(jnp.swapaxes(by_core(0, cut), 0, 1), "narrow", 1)
    parts = add_up(jnp.swapaxes(parts, 0, 1), "expert", CORES)
    left = last_pair(parts, 2)
    right = last_pair(add_up(by_core(cut, feature_len), "expert", CORES), 1)
    return finish([left, right], readout, pair_flags)


def solution(mesh):
    in_specs = (
        P(("groups", "expert", "narrow"), None),
        P(("groups", "expert"), None),
        P(("groups", "expert"), None),
        P(("groups", "expert", "narrow")),
        P(None, None, "narrow"),
        P("narrow", None),
        P("expert", None, None, "narrow"),
        P("expert", "narrow", None),
        P(),
    )
    out_specs = (P(("groups", "expert", "narrow"), None), P(("groups", "expert", "narrow")))
    return jax.shard_map(
        per_device, mesh=mesh, in_specs=in_specs, out_specs=out_specs, check_vma=False
    )
```

```python
import functools
import math

import jax
import jax.numpy as jnp
from jax import lax
from jax.experimental import pallas as pl
from jax.experimental.pallas import tpu as pltpu
from jax.sharding import PartitionSpec as P

ROT = 128
CORES = 2
SMALL_VMEM = 10 * 1024 * 1024
EARLY = 4
HIDDEN_VMEM = 5 * 1024 * 1024


def sign_matrix(copies):
    size = copies * ROT
    row_index = lax.broadcasted_iota(jnp.int32, (size, size), 0)
    col_index = lax.broadcasted_iota(jnp.int32, (size, size), 1)
    common = jnp.bitwise_and(row_index % ROT, col_index % ROT)
    parity = jnp.zeros((size, size), jnp.int32)
    for shift_bits in range(ROT.bit_length() - 1):
        parity = parity + jnp.bitwise_and(jnp.right_shift(common, shift_bits), 1)
    signs = 1 - 2 * jnp.bitwise_and(parity, 1)
    return jnp.where(row_index // ROT == col_index // ROT, signs, 0).astype(jnp.bfloat16)


def in_vmem(value):
    return pltpu.with_memory_space_constraint(value, pltpu.VMEM)


def vmem(shape, dtype):
    return pltpu.VMEM(shape, dtype)


def apart_kernel(experts, rows, chunk, n_in, *refs):
    source = refs[0]
    outs = refs[n_in : n_in + len(experts)]
    done, *own_out, held, sems = refs[n_in + len(experts) :]
    slots = held.shape[0]
    count = 2 * outs[0].shape[2] // 128
    pieces = [(n, step) for n in range(len(experts)) for step in range(outs[0].shape[1] // rows)]

    def copy(at):
        n, step = pieces[at]
        return pltpu.make_async_copy(
            source.at[experts[n], pl.ds(step * rows * count, rows * count)],
            held.at[at % slots],
            sems.at[at % slots],
        )

    own_copies = []
    for out in own_out:
        columns = pl.ds(refs[1][0] * out.shape[1], out.shape[1])
        own_copies.append(pltpu.make_async_copy(refs[2].at[:, columns], out, sems.at[slots]))
    for at in range(min(slots, len(pieces))):
        copy(at).start()
    for own_copy in own_copies:
        own_copy.start()
    for at, (n, step) in enumerate(pieces):
        copy(at).wait()
        for row in range(0, rows, chunk):
            pairs = held[at % slots, row * count : (row + chunk) * count, :]
            pairs = jnp.swapaxes(pairs.reshape(chunk, count, 128), 0, 1)
            here = slice(step * rows + row, step * rows + row + chunk)
            for q in range(count):
                outs[n][q % 2, here, (q // 2) * 128 : (q // 2 + 1) * 128] = pairs[q]
        if at + slots < len(pieces):
            copy(at + slots).start()
    for own_copy in own_copies:
        own_copy.wait()
    done[...] = jnp.zeros_like(done)


def apart(packed, experts, feature_len, inner, after, shared=None):
    count = 2 * inner // 128
    rows = feature_len // 8 if feature_len % 512 == 0 else feature_len
    chunk = 64 if rows % 64 == 0 else rows
    whole = pl.BlockSpec(memory_space=pltpu.VMEM)
    anywhere = pl.BlockSpec(memory_space=pl.ANY)
    inputs, specs, own = list(after), [anywhere] * len(after), []
    if shared is not None:
        index, columns, units = shared
        inputs = [index, columns] + inputs
        specs = [pl.BlockSpec(memory_space=pltpu.SMEM), anywhere] + specs
        own = [vmem((feature_len, units, 2, 128), columns.dtype)]
    out = pl.pallas_call(
        functools.partial(apart_kernel, experts, rows, chunk, 1 + len(inputs)),
        in_specs=[pl.BlockSpec(memory_space=pl.ANY)] + specs,
        out_specs=[whole] * (len(experts) + 1 + len(own)),
        out_shape=[vmem((2, feature_len, inner), packed.dtype)] * len(experts)
        + [jax.ShapeDtypeStruct((8, 128), jnp.float32)]
        + own,
        scratch_shapes=[
            pltpu.VMEM((8, rows * count, 128), packed.dtype),
            pltpu.SemaphoreType.DMA((9,)),
        ],
        compiler_params=pltpu.CompilerParams(vmem_limit_bytes=SMALL_VMEM),
        cost_estimate=pl.CostEstimate(flops=0, bytes_accessed=1024, transcendentals=0),
        name="apart",
    )(packed, *inputs)
    return out[: len(experts)], out[len(experts)], out[len(experts) + 1 :]


def pass_kernel(n_pieces, *refs):
    out = refs[-1]
    base = 0
    for piece in refs[:n_pieces]:
        out[base : base + piece.shape[0], :] = piece[...]
        base += piece.shape[0]


def pass_on(pieces, after):
    rows = sum(piece.shape[0] for piece in pieces)
    return pl.pallas_call(
        functools.partial(pass_kernel, len(pieces)),
        in_specs=[pl.BlockSpec(memory_space=pltpu.VMEM)] * len(pieces)
        + [pl.BlockSpec(memory_space=pl.ANY)] * len(after),
        out_specs=pl.BlockSpec(memory_space=pltpu.VMEM),
        out_shape=vmem((rows, pieces[0].shape[1]), pieces[0].dtype),
        compiler_params=pltpu.CompilerParams(vmem_limit_bytes=HIDDEN_VMEM),
        cost_estimate=pl.CostEstimate(flops=0, bytes_accessed=1024, transcendentals=0),
        name="pass_on",
    )(*pieces, *after)


def pack_kernel(rows, lanes, out):
    out[:, : rows.shape[1]] = rows[...]
    out[:, rows.shape[1] :] = lanes[...]


def pack(rows, lanes):
    whole = pl.BlockSpec(memory_space=pltpu.VMEM)
    return pl.pallas_call(
        pack_kernel,
        in_specs=[whole] * 2,
        out_specs=whole,
        out_shape=vmem((rows.shape[0], rows.shape[1] + lanes.shape[1]), rows.dtype),
        compiler_params=pltpu.CompilerParams(vmem_limit_bytes=HIDDEN_VMEM),
        cost_estimate=pl.CostEstimate(flops=0, bytes_accessed=1024, transcendentals=0),
        name="pack",
    )(rows, lanes)


def join_kernel(n_pieces, *refs):
    lanes, out, others = refs[n_pieces], refs[-2], refs[-1]
    feature_len = refs[0].shape[1]
    own = out.shape[0] - others.shape[0]
    base = 0
    for piece in refs[:n_pieces]:
        out[base : base + piece.shape[0], :feature_len] = piece[...]
        if base:
            others[base - own : base - own + piece.shape[0], :feature_len] = piece[...]
        base += piece.shape[0]
    out[:, feature_len:] = lanes[...]
    others[:, feature_len:] = lanes[own:, :]


def join(pieces, lanes, after):
    whole = pl.BlockSpec(memory_space=pltpu.VMEM)
    rows, own = lanes.shape[0], pieces[0].shape[0]
    columns = pieces[0].shape[1] + lanes.shape[1]
    return pl.pallas_call(
        functools.partial(join_kernel, len(pieces)),
        in_specs=[whole] * (len(pieces) + 1) + [pl.BlockSpec(memory_space=pl.ANY)] * len(after),
        out_specs=[whole] * 2,
        out_shape=[vmem((rows, columns), lanes.dtype), vmem((rows - own, columns), lanes.dtype)],
        compiler_params=pltpu.CompilerParams(vmem_limit_bytes=HIDDEN_VMEM),
        cost_estimate=pl.CostEstimate(flops=0, bytes_accessed=1024, transcendentals=0),
        name="join",
    )(*pieces, lanes, *after)


def rotate(sources, signs, target, bases):
    feature_len = target.shape[1]
    width = signs.shape[0]
    for at in range(0, feature_len, width):
        for source, base in zip(sources, bases):
            rotated = jnp.dot(
                source[:, at : at + width], signs[...], preferred_element_type=jnp.float32
            ) * (1.0 / math.sqrt(ROT))
            for piece_at in range(0, width, ROT):
                part = rotated[:, piece_at : piece_at + ROT]
                scale = jnp.max(jnp.abs(part), axis=1, keepdims=True) + 1e-06
                scale = scale.astype(jnp.bfloat16).astype(jnp.float32)
                quantized = (part * (1.0 / scale)).astype(jnp.bfloat16).astype(jnp.float32)
                target[
                    base : base + source.shape[0], at + piece_at : at + piece_at + ROT
                ] = (quantized * scale).astype(jnp.bfloat16)


def first_kernel(n_pieces, *refs):
    signs, out = refs[n_pieces:]
    pieces = refs[:n_pieces]
    rotate(pieces, signs, out, [n * pieces[0].shape[0] for n in range(n_pieces)])


def first_rows(pieces, signs, feature_len):
    whole = pl.BlockSpec(memory_space=pltpu.VMEM)
    rows = sum(piece.shape[0] for piece in pieces)
    return pl.pallas_call(
        functools.partial(first_kernel, len(pieces)),
        in_specs=[whole] * (len(pieces) + 1),
        out_specs=whole,
        out_shape=vmem((rows, feature_len), jnp.bfloat16),
        compiler_params=pltpu.CompilerParams(vmem_limit_bytes=HIDDEN_VMEM),
        cost_estimate=pl.CostEstimate(flops=0, bytes_accessed=1024, transcendentals=0),
        name="first_rows",
    )(*pieces, signs)


def shared_units(pieces, feature_len, shared, rows_s, out):
    base = 0
    for piece in pieces:
        rows_s[base : base + piece.shape[0], :] = piece[:, :feature_len]
        base += piece.shape[0]
    part = shared.shape[1] // 2
    both = jnp.dot(rows_s[...], shared[...], preferred_element_type=jnp.float32)
    gate, up = both[:, :part], both[:, part:]
    out[...] = (gate / (1.0 + jnp.exp(-gate)) * up).astype(jnp.bfloat16)


def second_kernel(n_pieces, *refs):
    pieces = refs[:n_pieces]
    signs, shared, out, units, rows_s = refs[n_pieces:]
    count = pieces[0].shape[0]
    rotate(pieces[CORES:], signs, out, [n * count for n in range(n_pieces - CORES)])
    shared_units(pieces, out.shape[1], shared, rows_s, units)


def second_rows(pieces, signs, shared):
    whole = pl.BlockSpec(memory_space=pltpu.VMEM)
    feature_len = shared.shape[0]
    count = pieces[0].shape[0]
    rows = len(pieces) * count
    return pl.pallas_call(
        functools.partial(second_kernel, len(pieces)),
        in_specs=[whole] * (len(pieces) + 2),
        out_specs=[whole] * 2,
        out_shape=[
            vmem((rows - CORES * count, feature_len), jnp.bfloat16),
            vmem((rows, shared.shape[1] // 2), jnp.bfloat16),
        ],
        scratch_shapes=[pltpu.VMEM((rows, feature_len), jnp.bfloat16)],
        compiler_params=pltpu.CompilerParams(vmem_limit_bytes=HIDDEN_VMEM + 2 * rows * feature_len),
        cost_estimate=pl.CostEstimate(flops=0, bytes_accessed=1024, transcendentals=0),
        name="second_rows",
    )(*pieces, signs, shared)


def rest_kernel(n_chips, *refs):
    n_pieces = CORES * n_chips
    index, pieces = refs[0], refs[1 : 1 + n_pieces]
    signs, first, second, units, shared, shared_down, *outs, rows_s, last_s, sem = refs[1 + n_pieces :]
    deq, shared_hidden, combine, shared_out = outs
    own = shared_out.shape[0]
    own = pl.ds(pl.multiple_of(index[0] * own, own), own)
    copy = pltpu.make_async_copy(shared_down.at[own], shared_out, sem)
    copy.start()
    count = pieces[0].shape[0]
    feature_len = deq.shape[1]
    last = pieces[CORES + n_chips - 1 :]
    shared_units(last, feature_len, shared, rows_s, last_s)
    sources, bases = [], []
    for core in range(CORES):
        for chip in range(n_chips):
            base = (core * n_chips + chip) * count
            here = slice(base, base + count)
            at = core if chip == 0 else CORES + core * (n_chips - 1) + chip - 1
            piece = pieces[at]
            if chip == 0:
                deq[here, :] = first[core * count : (core + 1) * count, :]
            elif core == 0:
                deq[here, :] = second[(chip - 1) * count : chip * count, :]
            else:
                sources.append(piece)
                bases.append(base)
            if chip and core:
                shared_hidden[here, :] = last_s[(chip - 1) * count : chip * count, :]
            else:
                shared_hidden[here, :] = units[at * count : (at + 1) * count, :]
            combine[here, :] = piece[:, feature_len:].astype(jnp.float32)
    rotate(sources, signs, deq, bases)
    copy.wait()


def rest_rows(index, pieces, signs, first, second, units, shared, shared_down, n_chips):
    whole = pl.BlockSpec(memory_space=pltpu.VMEM)
    rows = sum(piece.shape[0] for piece in pieces)
    last = (n_chips - 1) * pieces[0].shape[0]
    feature_len = first.shape[1]
    part = shared.shape[1] // 2
    return pl.pallas_call(
        functools.partial(rest_kernel, n_chips),
        in_specs=[pl.BlockSpec(memory_space=pltpu.SMEM)]
        + [whole] * (len(pieces) + 5)
        + [pl.BlockSpec(memory_space=pl.ANY)],
        out_specs=[whole] * 4,
        out_shape=[
            vmem((rows, feature_len), jnp.bfloat16),
            vmem((rows, part), jnp.bfloat16),
            vmem((rows, pieces[0].shape[1] - feature_len), jnp.float32),
            vmem((part, feature_len), shared_down.dtype),
        ],
        scratch_shapes=[
            pltpu.VMEM((last, feature_len), jnp.bfloat16),
            pltpu.VMEM((last, part), jnp.bfloat16),
            pltpu.SemaphoreType.DMA(()),
        ],
        compiler_params=pltpu.CompilerParams(vmem_limit_bytes=HIDDEN_VMEM + 2 * last * feature_len),
        name="rest_rows",
    )(index, *pieces, signs, first, second, units, shared, shared_down)


def hidden_kernel(experts, *refs):
    n = len(experts)
    deq, combine, select, down = refs[:4]
    weights, out = refs[4 : 4 + n], refs[4 + n]
    down_out, sems = refs[5 + n : 5 + 2 * n], refs[5 + 2 * n]
    inner = out.shape[1] // n
    copies = [
        pltpu.make_async_copy(down.at[local], down_out[at], sems.at[at])
        for at, local in enumerate(experts)
    ]
    for copy in copies:
        copy.start()
    for at, local in enumerate(experts):
        gate = jnp.dot(deq[...], weights[at][0], preferred_element_type=jnp.float32)
        up = jnp.dot(deq[...], weights[at][1], preferred_element_type=jnp.float32)
        weight = jnp.sum(combine[...] * select[local : local + 1, :], axis=1, keepdims=True)
        out[:, at * inner : (at + 1) * inner] = (
            gate / (1.0 + jnp.exp(-gate)) * up * weight
        ).astype(jnp.bfloat16)
    for copy in copies:
        copy.wait()


def hidden_rows(deq, combine, select, down, experts, weights):
    whole = pl.BlockSpec(memory_space=pltpu.VMEM)
    rows = deq.shape[0]
    n = len(experts)
    out = pl.pallas_call(
        functools.partial(hidden_kernel, experts),
        in_specs=[whole] * 3 + [pl.BlockSpec(memory_space=pl.ANY)] + [whole] * n,
        out_specs=[whole] * (1 + n),
        out_shape=[
            vmem((rows, n * weights[0].shape[2]), jnp.bfloat16),
            *[vmem(down.shape[1:], down.dtype)] * n,
        ],
        scratch_shapes=[pltpu.SemaphoreType.DMA((n,))],
        compiler_params=pltpu.CompilerParams(vmem_limit_bytes=HIDDEN_VMEM),
        name="hidden_rows",
    )(deq, combine, select, down, *weights)
    return out[0], list(out[1:])


def down_kernel(start, tile, n_hidden, *refs):
    hidden, (shared_hidden, shared_down), downs = (
        refs[:n_hidden],
        refs[n_hidden : n_hidden + 2],
        refs[n_hidden + 2 : -1],
    )
    out = refs[-1]
    inner = downs[0].shape[0]
    per = hidden[0].shape[1] // inner
    for at in range(0, out.shape[1], tile):
        columns = slice(start + at, start + at + tile)
        total = jnp.dot(
            shared_hidden[...], shared_down[:, columns], preferred_element_type=jnp.float32
        )
        for local, down in enumerate(downs):
            units = slice(local % per * inner, (local % per + 1) * inner)
            total += jnp.dot(
                hidden[local // per][:, units],
                down[:, columns],
                preferred_element_type=jnp.float32,
            )
        out[:, at : at + tile] = total.astype(out.dtype)


def down_rows(hidden, shared_hidden, downs, shared_down, start, stop):
    rows = shared_hidden.shape[0]
    tile = math.gcd(256, math.gcd(start, stop - start))
    whole = pl.BlockSpec(memory_space=pltpu.VMEM)
    return pl.pallas_call(
        functools.partial(down_kernel, start, tile, len(hidden)),
        in_specs=[whole] * (2 + len(hidden) + len(downs)),
        out_specs=whole,
        out_shape=vmem((rows, stop - start), jnp.bfloat16),
        compiler_params=pltpu.CompilerParams(vmem_limit_bytes=HIDDEN_VMEM),
        name="down_rows",
    )(*hidden, shared_hidden, shared_down, *downs)


def finish_kernel(n_parts, *refs):
    parts = refs[: 2 * n_parts]
    readout, flags, mixed, scores = refs[2 * n_parts :]
    rows, feature_len = mixed.shape
    pairs = scores.shape[1]
    at = 0
    dots = jnp.zeros((rows, 1), jnp.float32)
    squares = jnp.zeros((rows, 1), jnp.float32)
    for part, got in zip(parts[::2], parts[1::2]):
        total = part[...] + got[...].astype(jnp.float32)
        columns = slice(at, at + total.shape[1])
        mixed[:, columns] = total.astype(mixed.dtype)
        dots += jnp.sum(total * readout[:, columns], axis=1, keepdims=True)
        squares += jnp.sum(total * total, axis=1, keepdims=True)
        at += total.shape[1]
    row_score = dots / jnp.sqrt(squares * (1.0 / feature_len) + 1e-06)
    row = lax.broadcasted_iota(jnp.int32, (rows, pairs), 0)
    first = 2 * lax.broadcasted_iota(jnp.int32, (rows, pairs), 1)
    signed = jnp.where(row == first, row_score, jnp.where(row == first + 1, -row_score, 0.0))
    scores[...] = jnp.sum(signed, axis=0, keepdims=True) * (1 - 2 * flags[...]).astype(jnp.float32)


def finish(parts, readout, pair_flags):
    whole = pl.BlockSpec(memory_space=pltpu.VMEM)
    rows = parts[0][0].shape[0]
    flat = [term for part in parts for term in part]
    mixed, scores = pl.pallas_call(
        functools.partial(finish_kernel, len(parts)),
        in_specs=[whole] * (len(flat) + 2),
        out_specs=[whole] * 2,
        out_shape=[
            jax.ShapeDtypeStruct((rows, readout.shape[0]), jnp.bfloat16),
            jax.ShapeDtypeStruct((1, rows // 2), jnp.float32),
        ],
        compiler_params=pltpu.CompilerParams(vmem_limit_bytes=HIDDEN_VMEM),
        name="finish",
    )(*flat, readout.reshape(1, -1), pair_flags.reshape(1, -1))
    return mixed, scores.reshape(-1)


def exchange(value, axis, flip):
    return lax.ppermute(value, axis, [(i, i ^ flip) for i in range(lax.axis_size(axis))])


def per_device(
    tokens,
    expert_ids,
    route_weights,
    pair_flags,
    shared_gate_up,
    shared_down,
    expert_gate_up,
    expert_down,
    readout,
):
    own_rows, feature_len = tokens.shape
    n_local, _, _, inner = expert_gate_up.shape
    expert_count = lax.axis_size("expert")
    narrow_count = lax.axis_size("narrow")
    chips = expert_count // CORES
    experts = n_local * expert_count
    expert_at = lax.axis_index("expert")
    narrow_at = lax.axis_index("narrow")

    named = lax.broadcasted_iota(jnp.int32, (1, 1, experts), 2)
    combine = jnp.sum(
        jnp.where(expert_ids[:, :, None] == named, route_weights[:, :, None], 0.0), axis=1
    )
    high = combine.astype(jnp.bfloat16)
    low = (combine - high.astype(jnp.float32)).astype(jnp.bfloat16)
    columns = -(-2 * experts // 128) * 128
    lanes = jnp.pad(jnp.concatenate([high, low], axis=1), ((0, 0), (0, columns - 2 * experts)))
    lanes = lanes.reshape(narrow_count, own_rows, columns)
    order = narrow_at ^ jnp.arange(narrow_count)
    lanes = lanes[order].reshape(narrow_count * own_rows, columns)
    local_ids = expert_at * n_local + lax.broadcasted_iota(jnp.int32, (n_local, columns), 0)
    column = lax.broadcasted_iota(jnp.int32, (n_local, columns), 1)
    select = ((column == local_ids) | (column == local_ids + experts)).astype(jnp.float32)

    shared_len = shared_down.shape[0]
    part_len = shared_len // expert_count
    if part_len % 128 == 0:
        shared_out, index = shared_down, expert_at.reshape(1)
        columns_of = shared_gate_up.reshape(feature_len, 2, shared_len // 128, 128)
        columns_of = pltpu.with_memory_space_constraint(
            columns_of.transpose(0, 2, 1, 3), pltpu.HBM
        )
        shared = (index, columns_of, part_len // 128)
    else:
        mine = lax.broadcasted_iota(jnp.int32, (shared_len, 1), 0) // part_len == expert_at
        shared_in, index = shared_gate_up.reshape(feature_len, -1), jnp.zeros((1,), jnp.int32)
        shared_out = jnp.where(mine, shared_down, jnp.zeros_like(shared_down))
        shared = None
    signs = sign_matrix(2 if feature_len % (2 * ROT) == 0 else 1)

    packed = expert_gate_up.reshape(n_local, feature_len, 2, inner // 128, 128)
    packed = packed.transpose(0, 1, 3, 2, 4).reshape(n_local, -1, 128)
    packed = pltpu.with_memory_space_constraint(packed, pltpu.HBM)

    early = (n_local + EARLY - 1) // EARLY
    from_z = [exchange(tokens, "narrow", flip) for flip in range(1, narrow_count)]
    packed_own = pack(tokens, lanes[:own_rows])
    own_from_x = [exchange(packed_own, "expert", flip * CORES) for flip in range(1, chips)]
    weights, done, own = apart(
        packed, [0], feature_len, inner, [lanes, select, signs, index, packed_own], shared
    )
    for expert in range(1, early):
        more, done, _ = apart(packed, [expert], feature_len, inner, [done])
        weights = weights + more
    if own:
        shared_in = own[0].transpose(0, 2, 1, 3).reshape(feature_len, -1)
    along_z, others = join([tokens] + from_z, lanes, [done] + own_from_x)
    from_x = [exchange(others, "expert", flip * CORES) for flip in range(1, chips)]
    near = exchange(along_z, "expert", 1)
    after = [along_z]
    if n_local > early:
        late, done, _ = apart(
            packed, list(range(early, n_local)), feature_len, inner, after + [shared_in]
        )
        weights = weights + late
        after = [done]
    first = first_rows([along_z, near], signs, feature_len)
    from_x = [pass_on([own, part], after + [first]) for own, part in zip(own_from_x, from_x)]
    from_both = [exchange(part, "expert", 1) for part in from_x]
    second, units = second_rows([along_z, near] + from_x, signs, shared_in)

    shared_out = pltpu.with_memory_space_constraint(shared_out, pltpu.HBM)
    deq, shared_hidden, combine, shared_out = rest_rows(
        index,
        [along_z, near] + from_x + from_both,
        signs,
        first,
        second,
        units,
        shared_in,
        shared_out,
        chips,
    )
    down = pltpu.with_memory_space_constraint(expert_down, pltpu.HBM)
    hidden, downs = [], []
    for at in range(0, n_local, 2):
        part, down_part = hidden_rows(
            deq, combine, select, down, list(range(n_local))[at : at + 2], weights[at : at + 2]
        )
        hidden.append(part)
        downs += down_part

    half = own_rows * narrow_count * chips
    cut = feature_len // 256 // 2 * 256

    def by_core(start, stop):
        part = down_rows(hidden, shared_hidden, downs, shared_out, start, stop)
        near = exchange(part[half:], "expert", 1)
        total = part[:half].astype(jnp.float32) + near.astype(jnp.float32)
        return total.reshape(chips, narrow_count, own_rows, stop - start)

    def halve(parts, axis, step):
        pairs = parts.reshape(parts.shape[0] // 2, 2, *parts.shape[1:])
        got = exchange(pairs[:, 1].astype(jnp.bfloat16), axis, step)
        return pairs[:, 0] + got.astype(jnp.float32)

    def add_up(parts, axis, step):
        while parts.shape[0] > 1:
            parts, step = halve(parts, axis, step), 2 * step
        return parts[0]

    def last_pair(parts, step):
        while parts.shape[0] > 2:
            parts, step = halve(parts, "narrow", step), 2 * step
        return parts[0], exchange(parts[1].astype(jnp.bfloat16), "narrow", step)

    parts = halve(jnp.swapaxes(by_core(0, cut), 0, 1), "narrow", 1)
    parts = add_up(jnp.swapaxes(parts, 0, 1), "expert", CORES)
    left = last_pair(parts, 2)
    right = last_pair(add_up(by_core(cut, feature_len), "expert", CORES), 1)
    return finish([left, right], readout, pair_flags)


def solution(mesh):
    in_specs = (
        P(("groups", "expert", "narrow"), None),
        P(("groups", "expert"), None),
        P(("groups", "expert"), None),
        P(("groups", "expert", "narrow")),
        P(None, None, "narrow"),
        P("narrow", None),
        P("expert", None, None, "narrow"),
        P("expert", "narrow", None),
        P(),
    )
    out_specs = (P(("groups", "expert", "narrow"), None), P(("groups", "expert", "narrow")))
    return jax.shard_map(
        per_device, mesh=mesh, in_specs=in_specs, out_specs=out_specs, check_vma=False
    )
```
